256 devices in a mesh: ctx: 8 (over x, core), fsdp: 32 (over y, z).
Axes of the slice: x: 4, y: 4, z: 8, core: 2. Of those that a mesh axis runs over, the one named last changes fastest.
Arguments:
- tokens: bfloat16 [65536, 2560], P(('ctx', 'fsdp')), may hold values from -6 to 6
- w_in: bfloat16 [2560, 4352], P('fsdp'), may hold values from -0.125 to 0.125
- conv_weight: float32 [4, 4352], replicated, may hold values from -3 to 3
- log_decay: float32 [65536, 64], P('ctx', 'fsdp'), may hold values from -2 to 0, as said below
- norm_gain: float32 [4096], P('fsdp'), may hold values from 0.1 to 1.9
Outputs:
- layer_out: bfloat16 [65536, 4096], P('ctx', 'fsdp')
The draws below stay inside these ranges and needn't reach their ends.
Inputs may be any that keep to these rules, and one draw needn't show every extreme that they name: `log_decay`: log of a per-position, per-head decay.
All inputs are finite; a program needn't handle non-finite values.
Results may differ from the reference program's by a relative error of at most 0.0037.
Values may be sent and summed in bfloat16 or wider, within the bound.
A program may use at most 128 MiB of HBM per device.

```python
import math
import jax
import jax.numpy as jnp
from jax import lax

D = 2560
H = 64
P_SIZE = 64
N = 128
K = 4
Q = 256
CTX_LEN = 8192
SEQUENCE_LENGTH = 65536


def draw_log_decay(key, part):
    key = jax.random.fold_in(key, 7)
    random_keys = jax.random.split(key, 6)
    slow_cut = 5
    slow_heads = jax.random.randint(random_keys[0], (H,), 0, 10) < slow_cut
    slow_log = jax.random.uniform(random_keys[5], (H,), jnp.float32, math.log(1.0 / (16.0 * Q)), math.log(1.0 / (4.0 * Q)))
    baseline_rate = jnp.where(slow_heads, jnp.exp(slow_log), 1.0 / 40.0)
    jaggedness = jax.random.uniform(random_keys[1], (SEQUENCE_LENGTH, H), jnp.float32, 0.5, 1.5)
    shard_count = SEQUENCE_LENGTH // CTX_LEN
    shard_multiplier = jnp.exp(jax.random.uniform(random_keys[2], (shard_count, H), jnp.float32, -0.69, 0.69))
    shard_multiplier = jnp.repeat(shard_multiplier, CTX_LEN, axis=0)
    spike_locations = jax.random.randint(random_keys[3], (3,), 0, SEQUENCE_LENGTH)
    spike_depth = jnp.log(jax.random.uniform(random_keys[4], (3,), jnp.float32, 0.55, 0.8))
    spike_events = jnp.zeros((SEQUENCE_LENGTH,), jnp.float32).at[spike_locations].add(spike_depth)
    return -baseline_rate[None, :] * jaggedness * shard_multiplier + spike_events[:, None]


def shard_levels(own_key, dims, shards, low, largest):
    loudness = 1.0
    for position, blocks in shards:
        draws = jax.random.uniform(jax.random.fold_in(jax.random.fold_in(own_key, 6), position), (blocks,), jnp.float32, low / len(shards), largest / len(shards))
        loudness = loudness * jnp.repeat(jnp.exp(draws), dims[position] // blocks).reshape((-1,) + (1,) * (len(dims) - 1 - position))
    return loudness


def centred(rng, extent, width, most, pieces=(), held_as=jnp.bfloat16):
    array = width * jax.random.normal(rng, extent, jnp.float32)
    if pieces:
        array = array * shard_levels(rng, extent, pieces, -0.22, 0.18)
    return jnp.clip(array, -most, most).astype(held_as)


def setup_inputs(seed: int = 0) -> dict:
    arg_keys = jax.random.split(jax.random.key(seed), 6)
    return {
        "tokens": centred(arg_keys[0], (SEQUENCE_LENGTH, D), 1.0, 6.0, ((0, 256),)),
        "w_in": centred(arg_keys[1], (D, H * P_SIZE + 2 * N), D ** -0.5, 0.125, ((0, 32),)),
        "conv_weight": centred(arg_keys[2], (K, H * P_SIZE + 2 * N), K ** -0.5, 3.0, (), jnp.float32),
        "log_decay": draw_log_decay(jax.random.fold_in(arg_keys[5], 71), 0),
        "norm_gain": jnp.clip(1.0 + 0.18 * jax.random.normal(arg_keys[4], (H * P_SIZE,), jnp.float32), 0.1, 1.9),
    }


def advance_block(carried_state, block_inputs):
    inner_part, b_block, c_block, decay_block = block_inputs
    cumulative = jnp.cumsum(decay_block, axis=0)
    scores = jnp.dot(c_block, b_block.T, preferred_element_type=jnp.float32)
    lower_mask = jnp.arange(Q)[:, None] >= jnp.arange(Q)[None, :]
    differences = cumulative[:, None, :] - cumulative[None, :, :]
    decay_weights = jnp.where(lower_mask[:, :, None], jnp.exp(jnp.minimum(differences, 0.0)), 0.0)
    weighted = (scores[:, :, None] * decay_weights).astype(jnp.bfloat16)
    within = jnp.einsum('tsh,shp->thp', weighted.astype(jnp.float32), inner_part.astype(jnp.float32))
    from_state = jnp.exp(cumulative)[:, :, None] * jnp.einsum('tn,hpn->thp', c_block.astype(jnp.float32), carried_state, precision=lax.Precision.HIGHEST)
    end_weights = jnp.exp(cumulative[-1][None, :] - cumulative)
    scaled_inner = (inner_part.astype(jnp.float32) * end_weights[:, :, None]).astype(jnp.bfloat16)
    contribution = jnp.einsum('shp,sn->hpn', scaled_inner.astype(jnp.float32), b_block.astype(jnp.float32))
    next_state = jnp.exp(cumulative[-1])[:, None, None] * carried_state + contribution
    return (next_state, within + from_state)

def reference(tokens, w_in, conv_weight, log_decay, norm_gain):
    projected = jnp.dot(tokens, w_in, preferred_element_type=jnp.float32).astype(jnp.bfloat16)
    padded = jnp.concatenate([jnp.zeros((K - 1, projected.shape[1]), jnp.bfloat16), projected], axis=0)
    summed = jnp.zeros(projected.shape, jnp.float32)
    for offset in range(K):
        summed = summed + conv_weight[offset] * padded[offset:offset + SEQUENCE_LENGTH].astype(jnp.float32)
    conv_out = jax.nn.silu(summed).astype(jnp.bfloat16)
    blocks = SEQUENCE_LENGTH // Q
    inner_all = conv_out[:, :H * P_SIZE].reshape(blocks, Q, H, P_SIZE)
    b_all = conv_out[:, H * P_SIZE:H * P_SIZE + N].reshape(blocks, Q, N)
    c_all = conv_out[:, H * P_SIZE + N:].reshape(blocks, Q, N)
    decay_all = log_decay.reshape(blocks, Q, H)
    start_state = jnp.zeros((H, P_SIZE, N), jnp.float32)
    _, outputs = lax.scan(advance_block, start_state, (inner_all, b_all, c_all, decay_all))
    outputs = outputs.reshape(SEQUENCE_LENGTH, H, P_SIZE)
    mean_square = lax.optimization_barrier(jnp.mean(outputs * outputs, axis=-1, keepdims=True))
    normed = outputs * lax.rsqrt(mean_square + 1e-05) * norm_gain.reshape(H, P_SIZE)
    return normed.reshape(SEQUENCE_LENGTH, H * P_SIZE).astype(jnp.bfloat16)
```

```python
import functools

import jax
import jax.numpy as jnp
from jax import lax
from jax.experimental import pallas as pl
from jax.experimental.pallas import tpu as pltpu
from jax.sharding import PartitionSpec as P

H = 64
P_SIZE = 64
N = 128
Q = 256
HALO = 16
MESH = pl.DeviceIdType.MESH
F32 = jnp.float32
BF16 = jnp.bfloat16
epsilon = 1e-05

NT = (((1,), (1,)), ((), ()))
TN = (((0,), (0,)), ((), ()))


def split2(v):
    high = v.astype(BF16)
    low = (v - high.astype(F32)).astype(BF16)
    return high, low


def lane_of(shape):
    return lax.broadcasted_iota(jnp.int32, shape, 1)


def scan_kernel(
    n_ctx,
    blocks,
    proj,
    bc,
    decay,
    taps,
    gain,
    out,
    cum,
    inner,
    starts,
    offsets,
    within,
    halo,
    mine,
    carries,
    halo_sems,
    send_sems,
    recv_sems,
):
    me = lax.axis_index("ctx")
    barrier = pltpu.get_barrier_semaphore()
    for r in range(1, n_ctx):
        pl.semaphore_signal(
            barrier,
            inc=1,
            device_id={"ctx": lax.rem(me + r, n_ctx)},
            device_id_type=MESH,
        )

    upper = (
        lax.broadcasted_iota(jnp.int32, (Q, Q), 0)
        <= lax.broadcasted_iota(jnp.int32, (Q, Q), 1)
    ).astype(BF16)
    steps = decay[...].reshape(blocks * 8, Q)
    high, rest = split2(steps)
    lowest = (steps - high.astype(F32) - rest.astype(F32)).astype(BF16)
    total = jnp.dot(lowest, upper, preferred_element_type=F32)
    total = total + jnp.dot(rest, upper, preferred_element_type=F32)
    total = total + jnp.dot(high, upper, preferred_element_type=F32)
    cum[...] = total.reshape(blocks, 8, Q)

    pl.semaphore_wait(barrier, n_ctx - 1)
    rows = blocks * Q
    halo_copy = pltpu.make_async_remote_copy(
        src_ref=proj.at[pl.ds(rows - HALO, HALO)],
        dst_ref=halo,
        send_sem=halo_sems.at[0],
        recv_sem=halo_sems.at[1],
        device_id={"ctx": lax.rem(me + 1, n_ctx)},
        device_id_type=MESH,
    )
    halo_copy.start()
    halo_copy.wait()

    def by_position(block):
        rows_of = cum[block]
        both = jnp.concatenate(
            [
                jnp.broadcast_to(rows_of[h : h + 1], (P_SIZE, Q))
                for h in range(2)
            ],
            axis=0,
        )
        return both.T

    def states(block, carry):
        tail, state, offset = carry
        base = pl.multiple_of(block * Q, Q)
        current = proj[pl.ds(base, Q), :].astype(F32)
        window = jnp.concatenate([tail, current], axis=0)
        summed = taps[0:1] * window[5 : 5 + Q]
        for k in range(1, 4):
            summed = summed + taps[k : k + 1] * window[5 + k : 5 + k + Q]
        own = jax.nn.silu(summed).astype(BF16)
        inner[pl.ds(base, Q), :] = own
        positions = by_position(block)
        last = positions[Q - 1 : Q]
        scaled = (own.astype(F32) * jnp.exp(last - positions)).astype(BF16)
        b_part = bc[pl.ds(base, Q), :N]
        added = lax.dot_general(b_part, scaled, TN, preferred_element_type=F32)
        starts[block] = state
        offsets[block] = jnp.broadcast_to(offset, (8, N))
        return current[Q - 8 :], jnp.exp(last) * state + added, offset + last

    first = jnp.where(me == 0, 0.0, halo[...].astype(F32))[HALO - 8 :]
    _, state, offset = lax.fori_loop(
        0,
        blocks,
        states,
        (first, jnp.zeros((N, 2 * P_SIZE), F32), jnp.zeros((1, 2 * P_SIZE), F32)),
    )
    mine[0:N] = state
    mine[N : N + 8] = jnp.broadcast_to(jnp.exp(offset), (8, 2 * P_SIZE))

    def carry_copy(r):
        return pltpu.make_async_remote_copy(
            src_ref=mine,
            dst_ref=carries.at[r - 1],
            send_sem=send_sems.at[r - 1],
            recv_sem=recv_sems.at[r - 1],
            device_id={"ctx": lax.rem(me + r, n_ctx)},
            device_id_type=MESH,
        )

    for r in range(1, n_ctx):
        carry_copy(r).start()

    mask = lax.broadcasted_iota(jnp.int32, (Q, Q), 0) >= lax.broadcasted_iota(
        jnp.int32, (Q, Q), 1
    )
    first_head = lane_of((Q, 2 * P_SIZE)) < P_SIZE

    def inside(block, _):
        base = pl.multiple_of(block * Q, Q)
        b_part = bc[pl.ds(base, Q), :N]
        c_part = bc[pl.ds(base, Q), N:]
        own = inner[pl.ds(base, Q), :]
        scores = lax.dot_general(c_part, b_part, NT, preferred_element_type=F32)
        rows_of = cum[block]
        parts = []
        for h in range(2):
            along = rows_of[h : h + 1]
            down = jnp.broadcast_to(along, (2 * P_SIZE, Q)).T
            down = jnp.concatenate([down, down], axis=1)
            weights = jnp.exp(jnp.where(mask, down - along, -1e30))
            weighted = (scores * weights).astype(BF16)
            parts.append(jnp.dot(weighted, own, preferred_element_type=F32))
        within[pl.ds(base, Q), :] = jnp.where(first_head, parts[0], parts[1])
        return 0

    lax.fori_loop(0, blocks, inside, 0)

    for r in range(1, n_ctx):
        carry_copy(r).wait()
    carried = jnp.zeros((N, 2 * P_SIZE), F32)
    for r in range(n_ctx - 1, 0, -1):
        new = carries[r - 1, N : N + 1] * carried + carries[r - 1, 0:N]
        carried = jnp.where(me - r >= 0, new, carried)

    same_head = (
        lax.broadcasted_iota(jnp.int32, (2 * N, 2 * P_SIZE), 0) % (2 * P_SIZE)
        // P_SIZE
        == lane_of((2 * N, 2 * P_SIZE)) // P_SIZE
    )
    averaging = jnp.where(same_head, 1.0 / P_SIZE, 0.0).astype(BF16)

    def finish(block, _):
        base = pl.multiple_of(block * Q, Q)
        c_part = bc[pl.ds(base, Q), N:]
        state = starts[block] + jnp.exp(offsets[block, 0:1]) * carried
        from_state = jnp.dot(
            jnp.concatenate([c_part, c_part], axis=1),
            jnp.concatenate(split2(state), axis=0),
            preferred_element_type=F32,
        )
        value = within[pl.ds(base, Q), :] + jnp.exp(by_position(block)) * from_state
        squares = jnp.concatenate(split2(value * value), axis=1)
        mean = jnp.dot(squares, averaging, preferred_element_type=F32)
        normed = value * lax.rsqrt(mean + epsilon) * gain[0:1]
        out[pl.ds(base, Q), :] = normed.astype(BF16)
        return 0

    lax.fori_loop(0, blocks, finish, 0)


def scan(n_ctx, proj, bc, decay, taps, gain):
    rows = proj.shape[0]
    blocks = rows // Q
    width = 2 * P_SIZE
    vmem = pl.BlockSpec(memory_space=pltpu.VMEM)
    return pl.pallas_call(
        functools.partial(scan_kernel, n_ctx, blocks),
        out_shape=jax.ShapeDtypeStruct((rows, width), BF16),
        in_specs=[vmem] * 5,
        out_specs=vmem,
        scratch_shapes=[
            pltpu.VMEM((blocks, 8, Q), F32),
            pltpu.VMEM((rows, width), BF16),
            pltpu.VMEM((blocks, N, width), F32),
            pltpu.VMEM((blocks, 8, width), F32),
            pltpu.VMEM((rows, width), F32),
            pltpu.VMEM((HALO, width), BF16),
            pltpu.VMEM((N + 8, width), F32),
            pltpu.VMEM((n_ctx - 1, N + 8, width), F32),
            pltpu.SemaphoreType.DMA((2,)),
            pltpu.SemaphoreType.DMA((n_ctx - 1,)),
            pltpu.SemaphoreType.DMA((n_ctx - 1,)),
        ],
        compiler_params=pltpu.CompilerParams(
            collective_id=1, has_side_effects=True, vmem_limit_bytes=48 * 2**20
        ),
    )(proj, bc, decay, taps, gain)


def shifted(block, axis, distance):
    devices = range(lax.axis_size(axis))
    route = [(i - distance, i) for i in devices if i - distance in devices]
    return lax.ppermute(block, axis, route)


def scan_operands(log_decay, conv_weight, norm_gain):
    rows = log_decay.shape[0]
    blocks = rows // Q
    steps = log_decay.T.reshape(2, blocks, Q).transpose(1, 0, 2)
    steps = jnp.pad(steps, ((0, 0), (0, 6), (0, 0)))
    width = 2 * P_SIZE
    mine = lax.dynamic_slice_in_dim(
        conv_weight, lax.axis_index("fsdp") * width, width, axis=1
    )
    return steps, jnp.pad(mine, ((0, 4), (0, 0))), jnp.broadcast_to(norm_gain, (8, width))


def body(tokens, w_in, conv_weight, log_decay, norm_gain):
    tok_rows = tokens.shape[0]
    projected = jnp.dot(
        tokens,
        lax.all_gather(w_in, "fsdp", axis=0, tiled=True),
        preferred_element_type=F32,
    ).astype(BF16)
    heads = lax.all_to_all(
        projected[:, : H * P_SIZE], "fsdp", split_axis=1, concat_axis=0, tiled=True
    )
    state_part = projected[:, H * P_SIZE :]
    state_taps = conv_weight[:, H * P_SIZE :]
    rim = shifted(state_part[tok_rows - 3 :], ("ctx", "fsdp"), 1)
    extended = jnp.concatenate([rim, state_part], axis=0).astype(F32)
    summed = jnp.zeros((tok_rows, 2 * N), F32)
    for k in range(4):
        summed = summed + state_taps[k] * extended[k : k + tok_rows]
    state_rows = lax.all_gather(
        jax.nn.silu(summed).astype(BF16), "fsdp", axis=0, tiled=True
    )
    steps, taps, gain = scan_operands(log_decay, conv_weight, norm_gain)
    return scan(lax.axis_size("ctx"), heads, state_rows, steps, taps, gain)


def solution(mesh):
    placed = (P(("ctx", "fsdp"), None), P("fsdp", None), P(), P("ctx", "fsdp"), P("fsdp"))
    return jax.shard_map(
        body, mesh=mesh, in_specs=placed, out_specs=P("ctx", "fsdp"), check_vma=False
    )
```

```python
import functools

import jax
import jax.numpy as jnp
from jax import lax
from jax.experimental import pallas as pl
from jax.experimental.pallas import tpu as pltpu
from jax.sharding import PartitionSpec as P

H = 64
P_SIZE = 64
N = 128
Q = 256
HALO = 16
MESH = pl.DeviceIdType.MESH
F32 = jnp.float32
BF16 = jnp.bfloat16
epsilon = 1e-05

NT = (((1,), (1,)), ((), ()))
TN = (((0,), (0,)), ((), ()))


def split2(v):
    high = v.astype(BF16)
    low = (v - high.astype(F32)).astype(BF16)
    return high, low


def lane_of(shape):
    return lax.broadcasted_iota(jnp.int32, shape, 1)


def scan_kernel(
    n_ctx,
    blocks,
    proj,
    bc,
    decay,
    taps,
    gain,
    out,
    cum,
    inner,
    starts,
    offsets,
    within,
    halo,
    mine,
    carries,
    halo_sems,
    send_sems,
    recv_sems,
):
    me = lax.axis_index("ctx")
    barrier = pltpu.get_barrier_semaphore()
    for r in range(1, n_ctx):
        pl.semaphore_signal(
            barrier,
            inc=1,
            device_id={"ctx": lax.rem(me + r, n_ctx)},
            device_id_type=MESH,
        )

    upper = (
        lax.broadcasted_iota(jnp.int32, (Q, Q), 0)
        <= lax.broadcasted_iota(jnp.int32, (Q, Q), 1)
    ).astype(BF16)
    steps = decay[...].reshape(blocks * 8, Q)
    high, rest = split2(steps)
    lowest = (steps - high.astype(F32) - rest.astype(F32)).astype(BF16)
    total = jnp.dot(lowest, upper, preferred_element_type=F32)
    total = total + jnp.dot(rest, upper, preferred_element_type=F32)
    total = total + jnp.dot(high, upper, preferred_element_type=F32)
    cum[...] = total.reshape(blocks, 8, Q)

    pl.semaphore_wait(barrier, n_ctx - 1)
    rows = blocks * Q
    halo_copy = pltpu.make_async_remote_copy(
        src_ref=proj.at[pl.ds(rows - HALO, HALO)],
        dst_ref=halo,
        send_sem=halo_sems.at[0],
        recv_sem=halo_sems.at[1],
        device_id={"ctx": lax.rem(me + 1, n_ctx)},
        device_id_type=MESH,
    )
    halo_copy.start()
    halo_copy.wait()

    def by_position(block):
        rows_of = cum[block]
        both = jnp.concatenate(
            [
                jnp.broadcast_to(rows_of[h : h + 1], (P_SIZE, Q))
                for h in range(2)
            ],
            axis=0,
        )
        return both.T

    def states(block, carry):
        tail, state, offset = carry
        base = pl.multiple_of(block * Q, Q)
        current = proj[pl.ds(base, Q), :].astype(F32)
        window = jnp.concatenate([tail, current], axis=0)
        summed = taps[0:1] * window[5 : 5 + Q]
        for k in range(1, 4):
            summed = summed + taps[k : k + 1] * window[5 + k : 5 + k + Q]
        own = jax.nn.silu(summed).astype(BF16)
        inner[pl.ds(base, Q), :] = own
        positions = by_position(block)
        last = positions[Q - 1 : Q]
        scaled = (own.astype(F32) * jnp.exp(last - positions)).astype(BF16)
        b_part = bc[pl.ds(base, Q), :N]
        added = lax.dot_general(b_part, scaled, TN, preferred_element_type=F32)
        starts[block] = state
        offsets[block] = jnp.broadcast_to(offset, (8, N))
        return current[Q - 8 :], jnp.exp(last) * state + added, offset + last

    first = jnp.where(me == 0, 0.0, halo[...].astype(F32))[HALO - 8 :]
    _, state, offset = lax.fori_loop(
        0,
        blocks,
        states,
        (first, jnp.zeros((N, 2 * P_SIZE), F32), jnp.zeros((1, 2 * P_SIZE), F32)),
    )
    mine[0:N] = state
    mine[N : N + 8] = jnp.broadcast_to(jnp.exp(offset), (8, 2 * P_SIZE))

    def carry_copy(r):
        return pltpu.make_async_remote_copy(
            src_ref=mine,
            dst_ref=carries.at[r - 1],
            send_sem=send_sems.at[r - 1],
            recv_sem=recv_sems.at[r - 1],
            device_id={"ctx": lax.rem(me + r, n_ctx)},
            device_id_type=MESH,
        )

    for r in range(1, n_ctx):
        carry_copy(r).start()

    mask = lax.broadcasted_iota(jnp.int32, (Q, Q), 0) >= lax.broadcasted_iota(
        jnp.int32, (Q, Q), 1
    )
    first_head = lane_of((Q, 2 * P_SIZE)) < P_SIZE

    def inside(block, _):
        base = pl.multiple_of(block * Q, Q)
        b_part = bc[pl.ds(base, Q), :N]
        c_part = bc[pl.ds(base, Q), N:]
        own = inner[pl.ds(base, Q), :]
        scores = lax.dot_general(c_part, b_part, NT, preferred_element_type=F32)
        rows_of = cum[block]
        parts = []
        for h in range(2):
            along = rows_of[h : h + 1]
            down = jnp.broadcast_to(along, (2 * P_SIZE, Q)).T
            down = jnp.concatenate([down, down], axis=1)
            weights = jnp.exp(jnp.where(mask, down - along, -1e30))
            weighted = (scores * weights).astype(BF16)
            parts.append(jnp.dot(weighted, own, preferred_element_type=F32))
        within[pl.ds(base, Q), :] = jnp.where(first_head, parts[0], parts[1])
        return 0

    lax.fori_loop(0, blocks, inside, 0)

    for r in range(1, n_ctx):
        carry_copy(r).wait()
    carried = jnp.zeros((N, 2 * P_SIZE), F32)
    for r in range(n_ctx - 1, 0, -1):
        new = carries[r - 1, N : N + 1] * carried + carries[r - 1, 0:N]
        carried = jnp.where(me - r >= 0, new, carried)

    same_head = (
        lax.broadcasted_iota(jnp.int32, (2 * N, 2 * P_SIZE), 0) % (2 * P_SIZE)
        // P_SIZE
        == lane_of((2 * N, 2 * P_SIZE)) // P_SIZE
    )
    averaging = jnp.where(same_head, 1.0 / P_SIZE, 0.0).astype(BF16)

    def finish(block, _):
        base = pl.multiple_of(block * Q, Q)
        c_part = bc[pl.ds(base, Q), N:]
        state = starts[block] + jnp.exp(offsets[block, 0:1]) * carried
        from_state = jnp.dot(
            jnp.concatenate([c_part, c_part], axis=1),
            jnp.concatenate(split2(state), axis=0),
            preferred_element_type=F32,
        )
        value = within[pl.ds(base, Q), :] + jnp.exp(by_position(block)) * from_state
        squares = jnp.concatenate(split2(value * value), axis=1)
        mean = jnp.dot(squares, averaging, preferred_element_type=F32)
        normed = value * lax.rsqrt(mean + epsilon) * gain[0:1]
        out[pl.ds(base, Q), :] = normed.astype(BF16)
        return 0

    lax.fori_loop(0, blocks, finish, 0)


def scan(n_ctx, proj, bc, decay, taps, gain):
    rows = proj.shape[0]
    blocks = rows // Q
    width = 2 * P_SIZE
    vmem = pl.BlockSpec(memory_space=pltpu.VMEM)
    return pl.pallas_call(
        functools.partial(scan_kernel, n_ctx, blocks),
        out_shape=jax.ShapeDtypeStruct((rows, width), BF16),
        in_specs=[vmem] * 5,
        out_specs=vmem,
        scratch_shapes=[
            pltpu.VMEM((blocks, 8, Q), F32),
            pltpu.VMEM((rows, width), BF16),
            pltpu.VMEM((blocks, N, width), F32),
            pltpu.VMEM((blocks, 8, width), F32),
            pltpu.VMEM((rows, width), F32),
            pltpu.VMEM((HALO, width), BF16),
            pltpu.VMEM((N + 8, width), F32),
            pltpu.VMEM((n_ctx - 1, N + 8, width), F32),
            pltpu.SemaphoreType.DMA((2,)),
            pltpu.SemaphoreType.DMA((n_ctx - 1,)),
            pltpu.SemaphoreType.DMA((n_ctx - 1,)),
        ],
        compiler_params=pltpu.CompilerParams(
            collective_id=1, has_side_effects=True, vmem_limit_bytes=48 * 2**20
        ),
    )(proj, bc, decay, taps, gain)


NX, NY, NZ = 4, 4, 8
ROWS = 256
DEPTH = 2560
SHARD = 80
HEAD_COLUMNS = 1024
STATE_AT = 4096


def exchange_kernel(
    tokens,
    w_in,
    taps,
    proj,
    bc,
    tok,
    weights,
    state_weights,
    pieces,
    halo,
    own_sems,
    halo_sems,
    tok_send,
    tok_recv,
    shard_sems,
    x_send,
    x_recv,
    core_send,
    core_recv,
    ring_send,
    ring_recv,
    bc_send,
    bc_recv,
    out_send,
    out_recv,
):
    ctx = lax.axis_index("ctx")
    f = lax.axis_index("fsdp")
    x, c = ctx // 2, lax.rem(ctx, 2)
    y, z = f // NZ, lax.rem(f, NZ)

    def at(dx=0, dc=0, dy=0, dz=0):
        return {
            "ctx": lax.rem(x + dx, NX) * 2 + lax.rem(c + dc, 2),
            "fsdp": lax.rem(y + dy, NY) * NZ + lax.rem(z + dz, NZ),
        }

    def remote(source, target, send_sem, recv_sem, device):
        return pltpu.make_async_remote_copy(
            src_ref=source,
            dst_ref=target,
            send_sem=send_sem,
            recv_sem=recv_sem,
            device_id=device,
            device_id_type=MESH,
        )

    def settle(ref, sem):
        pltpu.make_async_copy(ref, ref, sem).wait()

    def columns(index):
        return pl.ds(pl.multiple_of(index * 128, 128), 128)

    def shard(index):
        return pl.ds(pl.multiple_of(index * SHARD, 16), SHARD)

    def block(index):
        return pl.ds(pl.multiple_of(index * Q, Q), Q)

    half = columns(c)
    other_half = columns(1 - c)
    devices = NY * NZ

    barrier = pltpu.get_barrier_semaphore()

    def greet(device):
        pl.semaphore_signal(barrier, inc=1, device_id=device, device_id_type=MESH)

    def greet_row(r, _):
        greet({"ctx": ctx, "fsdp": lax.rem(f + r, devices)})
        return 0

    lax.fori_loop(1, devices, greet_row, 0)
    for dx in range(1, NX):
        greet(at(dx=dx))
    greet(at(dc=1))
    greet(
        {
            "ctx": lax.rem(ctx + 2 * NX - (devices - f) // devices, 2 * NX),
            "fsdp": lax.rem(f + devices - 1, devices),
        }
    )
    own_tokens = pltpu.make_async_copy(tokens, tok.at[0], own_sems.at[0])
    own_tokens.start()
    own_column = NZ * y + lax.rem(2 * x + c + z, NZ)
    own_shard = pltpu.make_async_copy(
        w_in.at[:, columns(own_column)],
        weights.at[0, shard(f), half],
        own_sems.at[1],
    )
    own_shard.start()
    own_state_shard = pltpu.make_async_copy(
        w_in.at[:, columns(STATE_AT // 128 + c)],
        state_weights.at[shard(f), half],
        own_sems.at[2],
    )
    gives_state = lax.rem(z, NX) == x

    @pl.when(gives_state)
    def _():
        own_state_shard.start()

    pl.semaphore_wait(barrier, devices - 1 + NX - 1 + 2)

    def give_shard(r, _):
        other = lax.rem(f + r, devices)
        column = NZ * (other // NZ) + lax.rem(2 * x + c + lax.rem(other, NZ), NZ)
        remote(
            w_in.at[:, columns(column)],
            weights.at[0, shard(f), half],
            shard_sems.at[0],
            shard_sems.at[1],
            {"ctx": ctx, "fsdp": other},
        ).start()
        return 0

    def state_shard_copy(r):
        return remote(
            w_in.at[:, columns(STATE_AT // 128 + c)],
            state_weights.at[shard(f), half],
            shard_sems.at[2],
            shard_sems.at[3],
            {"ctx": ctx, "fsdp": lax.rem(f + r, devices)},
        )

    def give_state_shard(r, _):
        state_shard_copy(r).start()
        return 0

    lax.fori_loop(1, devices, give_shard, 0)

    def tok_copy(slot, part, dy, target):
        rows = pl.ds(part * (ROWS // 2), ROWS // 2)
        source = tokens.at[rows] if slot == 0 else tok.at[slot, rows]
        way = 0 if dy == 1 else 1
        return remote(
            source,
            tok.at[target, rows],
            tok_send.at[slot, way, part],
            tok_recv.at[target, part],
            at(dy=dy),
        )

    halo_copy = remote(
        tokens.at[pl.ds(ROWS - HALO, HALO)],
        halo,
        halo_sems.at[0],
        halo_sems.at[1],
        {
            "ctx": lax.rem(ctx + (f + 1) // devices, 2 * NX),
            "fsdp": lax.rem(f + 1, devices),
        },
    )
    halo_copy.start()
    tok_copy(0, 0, 1, 3).start()
    tok_copy(0, 1, 3, 1).start()
    tok_copy(0, 1, 1, 3).start()
    tok_copy(0, 0, 3, 1).start()

    @pl.when(gives_state)
    def _():
        lax.fori_loop(1, devices, give_state_shard, 0)

    def tok_arrived(slot, part):
        settle(tok.at[slot, pl.ds(part * (ROWS // 2), ROWS // 2)], tok_recv.at[slot, part])

    def x_copy(slot, dx, target, part):
        rows = pl.ds(0, DEPTH) if part is None else pl.ds(part * (DEPTH // 2), DEPTH // 2)
        way = 0 if dx == 1 else 1
        return remote(
            weights.at[slot, rows, half],
            weights.at[target, rows, half],
            x_send.at[slot, way],
            x_recv.at[target, 0 if part is None else part],
            at(dx=dx),
        )

    def core_copy(slot):
        return remote(
            weights.at[slot, :, half],
            weights.at[slot, :, half],
            core_send.at[slot],
            core_recv.at[slot],
            at(dc=1),
        )

    own_shard.wait()
    settle(
        weights.at[0, pl.ds(0, (devices - 1) * SHARD), half], shard_sems.at[1]
    )
    core_copy(0).start()
    x_copy(0, 1, 3, None).start()
    x_copy(0, 3, 1, None).start()

    @pl.when(gives_state)
    def _():
        own_state_shard.wait()
        settle(state_weights.at[pl.ds(0, 7 * SHARD), half], shard_sems.at[3])

    @pl.when(jnp.logical_not(gives_state))
    def _():
        settle(state_weights.at[pl.ds(0, 8 * SHARD), half], shard_sems.at[3])

    def give_plane(i, _):
        rows = shard(lax.rem(i, 8) // 2 * NZ + x + NX * lax.rem(i, 2))
        remote(
            state_weights.at[rows, half],
            state_weights.at[rows, half],
            shard_sems.at[4],
            shard_sems.at[5],
            at(dx=1 + i // 8),
        ).start()
        return 0

    lax.fori_loop(0, 24, give_plane, 0)

    tok_arrived(3, 0)
    tok_copy(3, 0, 1, 2).start()
    tok_arrived(1, 1)
    tok_copy(1, 1, 3, 2).start()

    settle(state_weights.at[pl.ds(0, 24 * SHARD), half], shard_sems.at[5])
    state_core = remote(
        state_weights.at[:, half],
        state_weights.at[:, half],
        core_send.at[4],
        core_recv.at[4],
        at(dc=1),
    )
    state_core.start()
    halo_copy.wait_recv()
    settle(state_weights.at[:, other_half], core_recv.at[4])

    own_tokens.wait()
    before = jnp.dot(halo[...], state_weights[...], preferred_element_type=F32)
    before = jnp.where(ctx + f == 0, 0.0, before.astype(BF16).astype(F32))
    here = jnp.dot(tok[0], state_weights[...], preferred_element_type=F32)
    window = jnp.concatenate(
        [before[HALO - 8 :], here.astype(BF16).astype(F32)], axis=0
    )
    summed = taps[0:1] * window[5 : 5 + ROWS]
    for k in range(1, 4):
        summed = summed + taps[k : k + 1] * window[5 + k : 5 + k + ROWS]
    bc[block(f), :] = jax.nn.silu(summed).astype(BF16)

    def bc_rows(t, k):
        return lax.rem(y + t, NY) * NZ + lax.rem(z + k, NZ)

    def ring_copy(k, way):
        rows = bc.at[block(bc_rows(0, k))]
        target = (k + 7) % 8 if way == 0 else k + 1
        return remote(
            rows,
            rows,
            ring_send.at[k, way],
            ring_recv.at[target],
            at(dz=1 if way == 0 else NZ - 1),
        )

    def bc_copy(t, k, way):
        index = bc_rows(t, k)
        if t == 0:
            rows, part = bc.at[block(index)], 0
        else:
            part = way
            rows = bc.at[
                pl.ds(pl.multiple_of(index * Q + part * (Q // 2), Q // 2), Q // 2)
            ]
        target = (3 if way == 0 else 1) if t == 0 else 2
        return remote(
            rows,
            rows,
            bc_send.at[t, k, way],
            bc_recv.at[target, k, part],
            at(dy=1 if way == 0 else NY - 1),
        )

    def ring_arrived(k):
        settle(bc.at[block(bc_rows(0, k))], ring_recv.at[k])

    def bc_on(k):
        bc_copy(0, k, 0).start()
        bc_copy(0, k, 1).start()

    ring_copy(0, 0).start()
    ring_copy(0, 1).start()
    bc_on(0)

    def out_piece(t, s, side):
        away = lax.rem(2 * lax.rem(x + s, NX) + side, NZ)
        rows = block(lax.rem(y + t, NY) * NZ + z)
        return pieces.at[t, s, :, pl.ds(side * 128, 128)], rows, away

    def multiply(t, s):
        product = jnp.dot(tok[t], weights[s], preferred_element_type=F32)
        pieces[t, s] = product.astype(BF16)
        for side in range(2):
            source, rows, away = out_piece(t, s, side)

            @pl.when(away == 0)
            def _():
                pltpu.make_async_copy(source, proj.at[rows], out_send.at[0, t]).start()

            @pl.when(away != 0)
            def _():
                remote(
                    source,
                    proj.at[rows],
                    out_send.at[away, t],
                    out_recv.at[away, t],
                    {"ctx": ctx, "fsdp": y * NZ + lax.rem(z + away, NZ)},
                ).start()

    def core_arrived(slot):
        settle(weights.at[slot, :, other_half], core_recv.at[slot])

    core_arrived(0)
    multiply(0, 0)
    ring_arrived(7)
    ring_copy(7, 0).start()
    ring_arrived(1)
    ring_copy(1, 1).start()
    bc_on(7)
    bc_on(1)
    tok_arrived(3, 1)
    multiply(3, 0)
    tok_arrived(1, 0)
    multiply(1, 0)
    ring_arrived(6)
    ring_copy(6, 0).start()
    ring_arrived(2)
    ring_copy(2, 1).start()
    bc_on(6)
    bc_on(2)
    settle(weights.at[3, :, half], x_recv.at[3, 0])
    x_copy(3, 1, 2, 0).start()
    core_copy(3).start()
    settle(weights.at[1, :, half], x_recv.at[1, 0])
    x_copy(1, 3, 2, 1).start()
    core_copy(1).start()
    core_arrived(3)
    multiply(0, 3)
    ring_arrived(5)
    ring_copy(5, 0).start()
    ring_arrived(3)
    bc_on(5)
    bc_on(3)
    core_arrived(1)
    multiply(0, 1)
    multiply(3, 3)
    multiply(3, 1)
    multiply(1, 3)
    multiply(1, 1)
    ring_arrived(4)
    bc_on(4)
    settle(weights.at[2, pl.ds(0, DEPTH // 2), half], x_recv.at[2, 0])
    settle(weights.at[2, pl.ds(DEPTH // 2, DEPTH // 2), half], x_recv.at[2, 1])
    core_copy(2).start()
    core_arrived(2)
    multiply(0, 2)
    multiply(3, 2)
    multiply(1, 2)
    tok_arrived(2, 0)
    tok_arrived(2, 1)
    multiply(2, 0)
    multiply(2, 3)
    multiply(2, 1)
    multiply(2, 2)

    for k in (0, 7, 1, 6, 2, 5, 3, 4):
        settle(bc.at[block(bc_rows(3, k))], bc_recv.at[3, k, 0])
        bc_copy(3, k, 0).start()
        settle(bc.at[block(bc_rows(1, k))], bc_recv.at[1, k, 0])
        bc_copy(1, k, 1).start()

    for k in range(8):
        for way in range(2):
            bc_copy(0, k, way).wait_send()
            bc_copy(3 if way == 0 else 1, k, way).wait_send()
            index = bc_rows(2, k)
            settle(
                bc.at[pl.ds(pl.multiple_of(index * Q + way * (Q // 2), Q // 2), Q // 2)],
                bc_recv.at[2, k, way],
            )
    for k, way in ((0, 0), (0, 1), (7, 0), (1, 1), (6, 0), (2, 1), (5, 0)):
        ring_copy(k, way).wait_send()
    for slot in range(4):
        core_copy(slot).wait_send()
    state_core.wait_send()
    x_copy(0, 1, 3, None).wait_send()
    x_copy(0, 3, 1, None).wait_send()
    x_copy(3, 1, 2, 0).wait_send()
    x_copy(1, 3, 2, 1).wait_send()
    for part in range(2):
        tok_copy(0, part, 1, 3).wait_send()
        tok_copy(0, part, 3, 1).wait_send()
    tok_copy(3, 0, 1, 2).wait_send()
    tok_copy(1, 1, 3, 2).wait_send()
    halo_copy.wait_send()
    settle(weights.at[0, pl.ds(0, (devices - 1) * SHARD), half], shard_sems.at[0])
    settle(state_weights.at[pl.ds(0, 24 * SHARD), half], shard_sems.at[4])

    @pl.when(gives_state)
    def _():
        settle(
            state_weights.at[pl.ds(0, (devices - 1) * SHARD), half], shard_sems.at[2]
        )

    for t in range(NY):
        rows = lax.rem(y + t, NY) * NZ
        settle(proj.at[block(rows + z)], out_send.at[0, t])
        for away in range(1, NZ):
            settle(proj.at[block(rows + z)], out_send.at[away, t])
            source = lax.rem(z + NZ - away, NZ)
            settle(proj.at[block(rows + source)], out_recv.at[away, t])


def exchange(tokens, w_in, taps):
    vmem = pl.BlockSpec(memory_space=pltpu.VMEM)
    dma = pltpu.SemaphoreType.DMA
    blocks = NY * NZ
    return pl.pallas_call(
        exchange_kernel,
        out_shape=[
            jax.ShapeDtypeStruct((blocks * Q, 2 * P_SIZE), BF16),
            jax.ShapeDtypeStruct((blocks * Q, 2 * N), BF16),
        ],
        in_specs=[vmem] * 3,
        out_specs=[vmem] * 2,
        scratch_shapes=[
            pltpu.VMEM((NY, ROWS, DEPTH), BF16),
            pltpu.VMEM((NX, DEPTH, 256), BF16),
            pltpu.VMEM((DEPTH, 2 * N), BF16),
            pltpu.VMEM((NY, NX, ROWS, 256), BF16),
            pltpu.VMEM((HALO, DEPTH), BF16),
            dma((3,)),
            dma((2,)),
            dma((4, 2, 2)),
            dma((4, 2)),
            dma((6,)),
            dma((4, 2)),
            dma((4, 2)),
            dma((5,)),
            dma((5,)),
            dma((8, 2)),
            dma((8,)),
            dma((4, 8, 2)),
            dma((4, 8, 2)),
            dma((8, 4)),
            dma((8, 4)),
        ],
        compiler_params=pltpu.CompilerParams(
            collective_id=2, has_side_effects=True, vmem_limit_bytes=48 * 2**20
        ),
    )(tokens, w_in, taps)


def scan_operands(log_decay, conv_weight, norm_gain):
    rows = log_decay.shape[0]
    blocks = rows // Q
    steps = log_decay.T.reshape(2, blocks, Q).transpose(1, 0, 2)
    steps = jnp.pad(steps, ((0, 0), (0, 6), (0, 0)))
    width = 2 * P_SIZE
    mine = lax.dynamic_slice_in_dim(
        conv_weight, lax.axis_index("fsdp") * width, width, axis=1
    )
    return steps, jnp.pad(mine, ((0, 4), (0, 0))), jnp.broadcast_to(norm_gain, (8, width))


def body(tokens, w_in, conv_weight, log_decay, norm_gain):
    state_taps = jnp.pad(conv_weight[:, STATE_AT:], ((0, 4), (0, 0)))
    heads, state_rows = exchange(tokens, w_in, state_taps)
    steps, taps, gain = scan_operands(log_decay, conv_weight, norm_gain)
    return scan(lax.axis_size("ctx"), heads, state_rows, steps, taps, gain)


def solution(mesh):
    placed = (P(("ctx", "fsdp"), None), P("fsdp", None), P(), P("ctx", "fsdp"), P("fsdp"))
    return jax.shard_map(
        body, mesh=mesh, in_specs=placed, out_specs=P("ctx", "fsdp"), check_vma=False
    )
```

```python
import functools

import jax
import jax.numpy as jnp
from jax import lax
from jax.experimental import pallas as pl
from jax.experimental.pallas import tpu as pltpu
from jax.sharding import PartitionSpec as P

H = 64
P_SIZE = 64
N = 128
Q = 256
HALO = 16
MESH = pl.DeviceIdType.MESH
F32 = jnp.float32
BF16 = jnp.bfloat16
epsilon = 1e-05

NT = (((1,), (1,)), ((), ()))
TN = (((0,), (0,)), ((), ()))


def split2(v):
    high = v.astype(BF16)
    low = (v - high.astype(F32)).astype(BF16)
    return high, low


def lane_of(shape):
    return lax.broadcasted_iota(jnp.int32, shape, 1)


def scan_kernel(
    n_ctx,
    blocks,
    proj,
    bc,
    decay,
    taps,
    gain,
    out,
    cum,
    inner,
    starts,
    offsets,
    within,
    halo,
    mine,
    carries,
    halo_sems,
    send_sems,
    recv_sems,
):
    me = lax.axis_index("ctx")
    barrier = pltpu.get_barrier_semaphore()
    for r in range(1, n_ctx):
        pl.semaphore_signal(
            barrier,
            inc=1,
            device_id={"ctx": lax.rem(me + r, n_ctx)},
            device_id_type=MESH,
        )

    upper = (
        lax.broadcasted_iota(jnp.int32, (Q, Q), 0)
        <= lax.broadcasted_iota(jnp.int32, (Q, Q), 1)
    ).astype(BF16)
    steps = decay[...].reshape(blocks * 8, Q)
    high, rest = split2(steps)
    lowest = (steps - high.astype(F32) - rest.astype(F32)).astype(BF16)
    total = jnp.dot(lowest, upper, preferred_element_type=F32)
    total = total + jnp.dot(rest, upper, preferred_element_type=F32)
    total = total + jnp.dot(high, upper, preferred_element_type=F32)
    cum[...] = total.reshape(blocks, 8, Q)

    pl.semaphore_wait(barrier, n_ctx - 1)
    rows = blocks * Q
    halo_copy = pltpu.make_async_remote_copy(
        src_ref=proj.at[pl.ds(rows - HALO, HALO)],
        dst_ref=halo,
        send_sem=halo_sems.at[0],
        recv_sem=halo_sems.at[1],
        device_id={"ctx": lax.rem(me + 1, n_ctx)},
        device_id_type=MESH,
    )
    halo_copy.start()
    halo_copy.wait()

    def by_position(block):
        rows_of = cum[block]
        both = jnp.concatenate(
            [
                jnp.broadcast_to(rows_of[h : h + 1], (P_SIZE, Q))
                for h in range(2)
            ],
            axis=0,
        )
        return both.T

    def states(block, carry):
        tail, state, offset = carry
        base = pl.multiple_of(block * Q, Q)
        current = proj[pl.ds(base, Q), :].astype(F32)
        window = jnp.concatenate([tail, current], axis=0)
        summed = taps[0:1] * window[5 : 5 + Q]
        for k in range(1, 4):
            summed = summed + taps[k : k + 1] * window[5 + k : 5 + k + Q]
        own = jax.nn.silu(summed).astype(BF16)
        inner[pl.ds(base, Q), :] = own
        positions = by_position(block)
        last = positions[Q - 1 : Q]
        scaled = (own.astype(F32) * jnp.exp(last - positions)).astype(BF16)
        b_part = bc[pl.ds(base, Q), :N]
        added = lax.dot_general(b_part, scaled, TN, preferred_element_type=F32)
        starts[block] = state
        offsets[block] = jnp.broadcast_to(offset, (8, N))
        return current[Q - 8 :], jnp.exp(last) * state + added, offset + last

    first = jnp.where(me == 0, 0.0, halo[...].astype(F32))[HALO - 8 :]
    _, state, offset = lax.fori_loop(
        0,
        blocks,
        states,
        (first, jnp.zeros((N, 2 * P_SIZE), F32), jnp.zeros((1, 2 * P_SIZE), F32)),
        unroll=4,
    )
    mine[0:N] = state
    mine[N : N + 8] = jnp.broadcast_to(jnp.exp(offset), (8, 2 * P_SIZE))

    def carry_copy(r):
        return pltpu.make_async_remote_copy(
            src_ref=mine,
            dst_ref=carries.at[r - 1],
            send_sem=send_sems.at[r - 1],
            recv_sem=recv_sems.at[r - 1],
            device_id={"ctx": lax.rem(me + r, n_ctx)},
            device_id_type=MESH,
        )

    for r in range(1, n_ctx):
        carry_copy(r).start()

    mask = lax.broadcasted_iota(jnp.int32, (Q, Q), 0) >= lax.broadcasted_iota(
        jnp.int32, (Q, Q), 1
    )
    first_head = lane_of((Q, 2 * P_SIZE)) < P_SIZE

    def inside(block, _):
        base = pl.multiple_of(block * Q, Q)
        b_part = bc[pl.ds(base, Q), :N]
        c_part = bc[pl.ds(base, Q), N:]
        own = inner[pl.ds(base, Q), :]
        scores = lax.dot_general(c_part, b_part, NT, preferred_element_type=F32)
        rows_of = cum[block]
        parts = []
        for h in range(2):
            along = rows_of[h : h + 1]
            down = jnp.broadcast_to(along, (2 * P_SIZE, Q)).T
            down = jnp.concatenate([down, down], axis=1)
            weights = jnp.exp(jnp.where(mask, down - along, -1e30))
            weighted = (scores * weights).astype(BF16)
            parts.append(jnp.dot(weighted, own, preferred_element_type=F32))
        within[pl.ds(base, Q), :] = jnp.where(first_head, parts[0], parts[1])
        return 0

    lax.fori_loop(0, blocks, inside, 0, unroll=4)

    for r in range(1, n_ctx):
        carry_copy(r).wait()
    carried = jnp.zeros((N, 2 * P_SIZE), F32)
    for r in range(n_ctx - 1, 0, -1):
        new = carries[r - 1, N : N + 1] * carried + carries[r - 1, 0:N]
        carried = jnp.where(me - r >= 0, new, carried)

    same_head = (
        lax.broadcasted_iota(jnp.int32, (2 * N, 2 * P_SIZE), 0) % (2 * P_SIZE)
        // P_SIZE
        == lane_of((2 * N, 2 * P_SIZE)) // P_SIZE
    )
    averaging = jnp.where(same_head, 1.0 / P_SIZE, 0.0).astype(BF16)

    def finish(block, _):
        base = pl.multiple_of(block * Q, Q)
        c_part = bc[pl.ds(base, Q), N:]
        state = starts[block] + jnp.exp(offsets[block, 0:1]) * carried
        from_state = jnp.dot(
            jnp.concatenate([c_part, c_part], axis=1),
            jnp.concatenate(split2(state), axis=0),
            preferred_element_type=F32,
        )
        value = within[pl.ds(base, Q), :] + jnp.exp(by_position(block)) * from_state
        squares = jnp.concatenate(split2(value * value), axis=1)
        mean = jnp.dot(squares, averaging, preferred_element_type=F32)
        normed = value * lax.rsqrt(mean + epsilon) * gain[0:1]
        out[pl.ds(base, Q), :] = normed.astype(BF16)
        return 0

    lax.fori_loop(0, blocks, finish, 0, unroll=4)


def scan(n_ctx, proj, bc, decay, taps, gain):
    rows = proj.shape[0]
    blocks = rows // Q
    width = 2 * P_SIZE
    vmem = pl.BlockSpec(memory_space=pltpu.VMEM)
    return pl.pallas_call(
        functools.partial(scan_kernel, n_ctx, blocks),
        out_shape=jax.ShapeDtypeStruct((rows, width), BF16),
        in_specs=[vmem] * 5,
        out_specs=vmem,
        scratch_shapes=[
            pltpu.VMEM((blocks, 8, Q), F32),
            pltpu.VMEM((rows, width), BF16),
            pltpu.VMEM((blocks, N, width), F32),
            pltpu.VMEM((blocks, 8, width), F32),
            pltpu.VMEM((rows, width), F32),
            pltpu.VMEM((HALO, width), BF16),
            pltpu.VMEM((N + 8, width), F32),
            pltpu.VMEM((n_ctx - 1, N + 8, width), F32),
            pltpu.SemaphoreType.DMA((2,)),
            pltpu.SemaphoreType.DMA((n_ctx - 1,)),
            pltpu.SemaphoreType.DMA((n_ctx - 1,)),
        ],
        compiler_params=pltpu.CompilerParams(
            collective_id=1, has_side_effects=True, vmem_limit_bytes=48 * 2**20
        ),
    )(proj, bc, decay, taps, gain)


NX, NY, NZ = 4, 4, 8
ROWS = 256
DEPTH = 2560
SHARD = 80
HEAD_COLUMNS = 1024
STATE_AT = 4096


def exchange_kernel(
    tokens,
    w_in,
    taps,
    proj,
    bc,
    tok,
    weights,
    state_weights,
    pieces,
    halo,
    own_sems,
    halo_sems,
    tok_send,
    tok_recv,
    shard_sems,
    x_send,
    x_recv,
    core_send,
    core_recv,
    ring_send,
    ring_recv,
    bc_send,
    bc_recv,
    out_send,
    out_recv,
):
    ctx = lax.axis_index("ctx")
    f = lax.axis_index("fsdp")
    x, c = ctx // 2, lax.rem(ctx, 2)
    y, z = f // NZ, lax.rem(f, NZ)

    def at(dx=0, dc=0, dy=0, dz=0):
        return {
            "ctx": lax.rem(x + dx, NX) * 2 + lax.rem(c + dc, 2),
            "fsdp": lax.rem(y + dy, NY) * NZ + lax.rem(z + dz, NZ),
        }

    def remote(source, target, send_sem, recv_sem, device):
        return pltpu.make_async_remote_copy(
            src_ref=source,
            dst_ref=target,
            send_sem=send_sem,
            recv_sem=recv_sem,
            device_id=device,
            device_id_type=MESH,
        )

    def settle(ref, sem):
        pltpu.make_async_copy(ref, ref, sem).wait()

    def columns(index):
        return pl.ds(pl.multiple_of(index * 128, 128), 128)

    def shard(index):
        return pl.ds(pl.multiple_of(index * SHARD, 16), SHARD)

    def block(index):
        return pl.ds(pl.multiple_of(index * Q, Q), Q)

    half = columns(c)
    other_half = columns(1 - c)
    devices = NY * NZ

    barrier = pltpu.get_barrier_semaphore()

    def greet(device):
        pl.semaphore_signal(barrier, inc=1, device_id=device, device_id_type=MESH)

    def greet_row(r, _):
        greet({"ctx": ctx, "fsdp": lax.rem(f + r, devices)})
        return 0

    lax.fori_loop(1, devices, greet_row, 0)
    for dx in range(1, NX):
        greet(at(dx=dx))
    greet(at(dc=1))
    greet(
        {
            "ctx": lax.rem(ctx + 2 * NX - (devices - f) // devices, 2 * NX),
            "fsdp": lax.rem(f + devices - 1, devices),
        }
    )
    own_tokens = pltpu.make_async_copy(tokens, tok.at[0], own_sems.at[0])
    own_tokens.start()
    own_column = NZ * y + lax.rem(2 * x + c + z, NZ)
    own_shard = pltpu.make_async_copy(
        w_in.at[:, columns(own_column)],
        weights.at[0, shard(f), half],
        own_sems.at[1],
    )
    own_shard.start()
    own_state_shard = pltpu.make_async_copy(
        w_in.at[:, columns(STATE_AT // 128 + c)],
        state_weights.at[shard(f), half],
        own_sems.at[2],
    )
    gives_state = lax.rem(z, NX) == x

    @pl.when(gives_state)
    def _():
        own_state_shard.start()

    pl.semaphore_wait(barrier, devices - 1 + NX - 1 + 2)

    def give_shard(r, _):
        other = lax.rem(f + r, devices)
        column = NZ * (other // NZ) + lax.rem(2 * x + c + lax.rem(other, NZ), NZ)
        remote(
            w_in.at[:, columns(column)],
            weights.at[0, shard(f), half],
            shard_sems.at[0],
            shard_sems.at[1],
            {"ctx": ctx, "fsdp": other},
        ).start()
        return 0

    def state_shard_copy(r):
        return remote(
            w_in.at[:, columns(STATE_AT // 128 + c)],
            state_weights.at[shard(f), half],
            shard_sems.at[2],
            shard_sems.at[3],
            {"ctx": ctx, "fsdp": lax.rem(f + r, devices)},
        )

    def give_state_shard(r, _):
        state_shard_copy(r).start()
        return 0

    @pl.when(gives_state)
    def _():
        lax.fori_loop(1, devices, give_state_shard, 0)

    lax.fori_loop(1, devices, give_shard, 0)

    def tok_copy(slot, part, dy, target):
        rows = pl.ds(part * (ROWS // 2), ROWS // 2)
        source = tokens.at[rows] if slot == 0 else tok.at[slot, rows]
        way = 0 if dy == 1 else 1
        return remote(
            source,
            tok.at[target, rows],
            tok_send.at[slot, way, part],
            tok_recv.at[target, part],
            at(dy=dy),
        )

    halo_copy = remote(
        tokens.at[pl.ds(ROWS - HALO, HALO)],
        halo,
        halo_sems.at[0],
        halo_sems.at[1],
        {
            "ctx": lax.rem(ctx + (f + 1) // devices, 2 * NX),
            "fsdp": lax.rem(f + 1, devices),
        },
    )
    halo_copy.start()
    tok_copy(0, 0, 1, 3).start()
    tok_copy(0, 1, 3, 1).start()
    tok_copy(0, 1, 1, 3).start()
    tok_copy(0, 0, 3, 1).start()

    def tok_arrived(slot, part):
        settle(tok.at[slot, pl.ds(part * (ROWS // 2), ROWS // 2)], tok_recv.at[slot, part])

    def x_copy(slot, dx, target, part):
        rows = pl.ds(0, DEPTH) if part is None else pl.ds(part * (DEPTH // 2), DEPTH // 2)
        way = 0 if dx == 1 else 1
        return remote(
            weights.at[slot, rows, half],
            weights.at[target, rows, half],
            x_send.at[slot, way],
            x_recv.at[target, 0 if part is None else part],
            at(dx=dx),
        )

    def core_copy(slot):
        return remote(
            weights.at[slot, :, half],
            weights.at[slot, :, half],
            core_send.at[slot],
            core_recv.at[slot],
            at(dc=1),
        )

    def bc_rows(t, k):
        return lax.rem(y + t, NY) * NZ + lax.rem(z + k, NZ)

    def ring_copy(k, way):
        rows = bc.at[block(bc_rows(0, k))]
        target = (k + 7) % 8 if way == 0 else k + 1
        return remote(
            rows,
            rows,
            ring_send.at[k, way],
            ring_recv.at[target],
            at(dz=1 if way == 0 else NZ - 1),
        )

    def bc_copy(t, k, way):
        index = bc_rows(t, k)
        if t == 0:
            rows, part = bc.at[block(index)], 0
        else:
            part = way
            rows = bc.at[
                pl.ds(pl.multiple_of(index * Q + part * (Q // 2), Q // 2), Q // 2)
            ]
        target = (3 if way == 0 else 1) if t == 0 else 2
        return remote(
            rows,
            rows,
            bc_send.at[t, k, way],
            bc_recv.at[target, k, part],
            at(dy=1 if way == 0 else NY - 1),
        )

    def ring_arrived(k):
        settle(bc.at[block(bc_rows(0, k))], ring_recv.at[k])

    def bc_on(k):
        bc_copy(0, k, 0).start()
        bc_copy(0, k, 1).start()

    def out_piece(t, s, side):
        away = lax.rem(2 * lax.rem(x + s, NX) + side, NZ)
        rows = block(lax.rem(y + t, NY) * NZ + z)
        return pieces.at[t, s, :, pl.ds(side * 128, 128)], rows, away

    def multiply(t, s):
        product = jnp.dot(tok[t], weights[s], preferred_element_type=F32)
        pieces[t, s] = product.astype(BF16)
        for side in range(2):
            source, rows, away = out_piece(t, s, side)

            @pl.when(away == 0)
            def _():
                pltpu.make_async_copy(source, proj.at[rows], out_send.at[0, t]).start()

            @pl.when(away != 0)
            def _():
                remote(
                    source,
                    proj.at[rows],
                    out_send.at[away, t],
                    out_recv.at[away, t],
                    {"ctx": ctx, "fsdp": y * NZ + lax.rem(z + away, NZ)},
                ).start()

    def core_arrived(slot):
        settle(weights.at[slot, :, other_half], core_recv.at[slot])

    @pl.when(gives_state)
    def _():
        own_state_shard.wait()
        settle(state_weights.at[pl.ds(0, 7 * SHARD), half], shard_sems.at[3])

    @pl.when(jnp.logical_not(gives_state))
    def _():
        settle(state_weights.at[pl.ds(0, 8 * SHARD), half], shard_sems.at[3])

    def give_plane(i, _):
        rows = shard(lax.rem(i, 8) // 2 * NZ + x + NX * lax.rem(i, 2))
        remote(
            state_weights.at[rows, half],
            state_weights.at[rows, half],
            shard_sems.at[4],
            shard_sems.at[5],
            at(dx=1 + i // 8),
        ).start()
        return 0

    lax.fori_loop(0, 24, give_plane, 0)

    settle(state_weights.at[pl.ds(0, 24 * SHARD), half], shard_sems.at[5])
    state_core = remote(
        state_weights.at[:, half],
        state_weights.at[:, half],
        core_send.at[4],
        core_recv.at[4],
        at(dc=1),
    )
    state_core.start()
    own_tokens.wait()
    halo_copy.wait_recv()
    settle(state_weights.at[:, other_half], core_recv.at[4])

    before = jnp.dot(halo[...], state_weights[...], preferred_element_type=F32)
    before = jnp.where(ctx + f == 0, 0.0, before.astype(BF16).astype(F32))
    here = jnp.dot(tok[0], state_weights[...], preferred_element_type=F32)
    window = jnp.concatenate(
        [before[HALO - 8 :], here.astype(BF16).astype(F32)], axis=0
    )
    summed = taps[0:1] * window[5 : 5 + ROWS]
    for k in range(1, 4):
        summed = summed + taps[k : k + 1] * window[5 + k : 5 + k + ROWS]
    bc[block(f), :] = jax.nn.silu(summed).astype(BF16)

    ring_copy(0, 0).start()
    ring_copy(0, 1).start()
    own_shard.wait()
    settle(
        weights.at[0, pl.ds(0, (devices - 1) * SHARD), half], shard_sems.at[1]
    )
    core_copy(0).start()
    x_copy(0, 1, 3, None).start()
    x_copy(0, 3, 1, None).start()

    tok_arrived(3, 0)
    tok_copy(3, 0, 1, 2).start()
    tok_arrived(1, 1)
    tok_copy(1, 1, 3, 2).start()

    ring_arrived(7)
    ring_copy(7, 0).start()
    ring_arrived(1)
    ring_copy(1, 1).start()
    core_arrived(0)
    multiply(0, 0)
    bc_on(0)
    bc_on(7)
    bc_on(1)
    ring_arrived(6)
    ring_copy(6, 0).start()
    ring_arrived(2)
    ring_copy(2, 1).start()
    bc_on(6)
    bc_on(2)
    ring_arrived(5)
    ring_copy(5, 0).start()
    ring_arrived(3)
    bc_on(5)
    bc_on(3)
    ring_arrived(4)
    bc_on(4)
    tok_arrived(3, 1)
    multiply(3, 0)
    tok_arrived(1, 0)
    multiply(1, 0)
    settle(weights.at[3, :, half], x_recv.at[3, 0])
    x_copy(3, 1, 2, 0).start()
    core_copy(3).start()
    settle(weights.at[1, :, half], x_recv.at[1, 0])
    x_copy(1, 3, 2, 1).start()
    core_copy(1).start()
    core_arrived(3)
    multiply(0, 3)
    multiply(3, 3)
    multiply(1, 3)
    core_arrived(1)
    multiply(0, 1)
    multiply(3, 1)
    multiply(1, 1)
    settle(weights.at[2, pl.ds(0, DEPTH // 2), half], x_recv.at[2, 0])
    settle(weights.at[2, pl.ds(DEPTH // 2, DEPTH // 2), half], x_recv.at[2, 1])
    core_copy(2).start()
    core_arrived(2)
    multiply(0, 2)
    multiply(3, 2)
    multiply(1, 2)
    tok_arrived(2, 0)
    tok_arrived(2, 1)
    multiply(2, 0)
    multiply(2, 3)
    multiply(2, 1)
    multiply(2, 2)

    for k in (0, 7, 1, 6, 2, 5, 3, 4):
        settle(bc.at[block(bc_rows(3, k))], bc_recv.at[3, k, 0])
        bc_copy(3, k, 0).start()
        settle(bc.at[block(bc_rows(1, k))], bc_recv.at[1, k, 0])
        bc_copy(1, k, 1).start()

    for k in range(8):
        for way in range(2):
            bc_copy(0, k, way).wait_send()
            bc_copy(3 if way == 0 else 1, k, way).wait_send()
            index = bc_rows(2, k)
            settle(
                bc.at[pl.ds(pl.multiple_of(index * Q + way * (Q // 2), Q // 2), Q // 2)],
                bc_recv.at[2, k, way],
            )
    for k, way in ((0, 0), (0, 1), (7, 0), (1, 1), (6, 0), (2, 1), (5, 0)):
        ring_copy(k, way).wait_send()
    for slot in range(4):
        core_copy(slot).wait_send()
    state_core.wait_send()
    x_copy(0, 1, 3, None).wait_send()
    x_copy(0, 3, 1, None).wait_send()
    x_copy(3, 1, 2, 0).wait_send()
    x_copy(1, 3, 2, 1).wait_send()
    for part in range(2):
        tok_copy(0, part, 1, 3).wait_send()
        tok_copy(0, part, 3, 1).wait_send()
    tok_copy(3, 0, 1, 2).wait_send()
    tok_copy(1, 1, 3, 2).wait_send()
    halo_copy.wait_send()
    settle(weights.at[0, pl.ds(0, (devices - 1) * SHARD), half], shard_sems.at[0])
    settle(state_weights.at[pl.ds(0, 24 * SHARD), half], shard_sems.at[4])

    @pl.when(gives_state)
    def _():
        settle(
            state_weights.at[pl.ds(0, (devices - 1) * SHARD), half], shard_sems.at[2]
        )

    for t in range(NY):
        rows = lax.rem(y + t, NY) * NZ
        settle(proj.at[block(rows + z)], out_send.at[0, t])
        for away in range(1, NZ):
            settle(proj.at[block(rows + z)], out_send.at[away, t])
            source = lax.rem(z + NZ - away, NZ)
            settle(proj.at[block(rows + source)], out_recv.at[away, t])


def exchange(tokens, w_in, taps):
    vmem = pl.BlockSpec(memory_space=pltpu.VMEM)
    dma = pltpu.SemaphoreType.DMA
    blocks = NY * NZ
    return pl.pallas_call(
        exchange_kernel,
        out_shape=[
            jax.ShapeDtypeStruct((blocks * Q, 2 * P_SIZE), BF16),
            jax.ShapeDtypeStruct((blocks * Q, 2 * N), BF16),
        ],
        in_specs=[vmem] * 3,
        out_specs=[vmem] * 2,
        scratch_shapes=[
            pltpu.VMEM((NY, ROWS, DEPTH), BF16),
            pltpu.VMEM((NX, DEPTH, 256), BF16),
            pltpu.VMEM((DEPTH, 2 * N), BF16),
            pltpu.VMEM((NY, NX, ROWS, 256), BF16),
            pltpu.VMEM((HALO, DEPTH), BF16),
            dma((3,)),
            dma((2,)),
            dma((4, 2, 2)),
            dma((4, 2)),
            dma((6,)),
            dma((4, 2)),
            dma((4, 2)),
            dma((5,)),
            dma((5,)),
            dma((8, 2)),
            dma((8,)),
            dma((4, 8, 2)),
            dma((4, 8, 2)),
            dma((8, 4)),
            dma((8, 4)),
        ],
        compiler_params=pltpu.CompilerParams(
            collective_id=2, has_side_effects=True, vmem_limit_bytes=48 * 2**20
        ),
    )(tokens, w_in, taps)


def scan_operands(log_decay, conv_weight, norm_gain):
    rows = log_decay.shape[0]
    blocks = rows // Q
    steps = log_decay.T.reshape(2, blocks, Q).transpose(1, 0, 2)
    steps = jnp.pad(steps, ((0, 0), (0, 6), (0, 0)))
    width = 2 * P_SIZE
    mine = lax.dynamic_slice_in_dim(
        conv_weight, lax.axis_index("fsdp") * width, width, axis=1
    )
    return steps, jnp.pad(mine, ((0, 4), (0, 0))), jnp.broadcast_to(norm_gain, (8, width))


def body(tokens, w_in, conv_weight, log_decay, norm_gain):
    state_taps = jnp.pad(conv_weight[:, STATE_AT:], ((0, 4), (0, 0)))
    heads, state_rows = exchange(tokens, w_in, state_taps)
    steps, taps, gain = scan_operands(log_decay, conv_weight, norm_gain)
    return scan(lax.axis_size("ctx"), heads, state_rows, steps, taps, gain)


def solution(mesh):
    placed = (P(("ctx", "fsdp"), None), P("fsdp", None), P(), P("ctx", "fsdp"), P("fsdp"))
    return jax.shard_map(
        body, mesh=mesh, in_specs=placed, out_specs=P("ctx", "fsdp"), check_vma=False
    )
```

```python
import jax
import jax.numpy as jnp
from jax import lax
from jax.experimental import pallas as pl
from jax.experimental.pallas import tpu as pltpu
from jax.sharding import PartitionSpec as P

H = 64
P_SIZE = 64
N = 128
Q = 256
HALO = 16
MESH = pl.DeviceIdType.MESH
F32 = jnp.float32
BF16 = jnp.bfloat16
epsilon = 1e-05

NT = (((1,), (1,)), ((), ()))
TN = (((0,), (0,)), ((), ()))


def split2(v):
    high = v.astype(BF16)
    low = (v - high.astype(F32)).astype(BF16)
    return high, low


def lane_of(shape):
    return lax.broadcasted_iota(jnp.int32, shape, 1)


NX, NY, NZ = 4, 4, 8
ROWS = 256
DEPTH = 2560
SHARD = 80
BLOCKS = NY * NZ
WIDTH = 2 * P_SIZE
STATE_AT = 4096


def layer_kernel(
    tokens,
    w_in,
    conv,
    decay,
    gain,
    out,
    proj,
    bc,
    cum,
    inner,
    starts,
    lasts,
    offsets,
    within,
    mine,
    carries,
    tok,
    weights,
    state_weights,
    pieces,
    halo,
    own_sems,
    halo_sems,
    tok_send,
    tok_recv,
    shard_sems,
    x_send,
    x_recv,
    core_send,
    core_recv,
    ring_send,
    ring_recv,
    bc_send,
    bc_recv,
    out_send,
    out_recv,
    edge_sems,
    carry_send,
    carry_recv,
):
    ctx = lax.axis_index("ctx")
    f = lax.axis_index("fsdp")
    x, c = ctx // 2, lax.rem(ctx, 2)
    y, z = f // NZ, lax.rem(f, NZ)

    def at(dx=0, dc=0, dy=0, dz=0):
        return {
            "ctx": lax.rem(x + dx, NX) * 2 + lax.rem(c + dc, 2),
            "fsdp": lax.rem(y + dy, NY) * NZ + lax.rem(z + dz, NZ),
        }

    def remote(source, target, send_sem, recv_sem, device):
        return pltpu.make_async_remote_copy(
            src_ref=source,
            dst_ref=target,
            send_sem=send_sem,
            recv_sem=recv_sem,
            device_id=device,
            device_id_type=MESH,
        )

    def settle(ref, sem):
        pltpu.make_async_copy(ref, ref, sem).wait()

    def columns(index):
        return pl.ds(pl.multiple_of(index * 128, 128), 128)

    def shard(index):
        return pl.ds(pl.multiple_of(index * SHARD, 16), SHARD)

    def block(index):
        return pl.ds(pl.multiple_of(index * Q, Q), Q)

    def positions(index):
        return pl.ds(pl.multiple_of(index * Q + HALO, HALO), Q)

    half = columns(c)
    other_half = columns(1 - c)
    devices = NY * NZ

    barrier = pltpu.get_barrier_semaphore()

    def greet(device):
        pl.semaphore_signal(barrier, inc=1, device_id=device, device_id_type=MESH)

    def greet_row(r, _):
        greet({"ctx": ctx, "fsdp": lax.rem(f + r, devices)})
        return 0

    lax.fori_loop(1, devices, greet_row, 0)
    for r in range(1, 2 * NX):
        greet({"ctx": lax.rem(ctx + r, 2 * NX), "fsdp": f})
    greet(
        {
            "ctx": lax.rem(ctx + 2 * NX - (devices - f) // devices, 2 * NX),
            "fsdp": lax.rem(f + devices - 1, devices),
        }
    )
    own_tokens = pltpu.make_async_copy(tokens, tok.at[0], own_sems.at[0])
    own_tokens.start()
    own_column = NZ * y + lax.rem(2 * x + c + z, NZ)
    own_shard = pltpu.make_async_copy(
        w_in.at[:, columns(own_column)],
        weights.at[0, shard(f), half],
        own_sems.at[1],
    )
    own_shard.start()
    own_state_shard = pltpu.make_async_copy(
        w_in.at[:, columns(STATE_AT // 128 + c)],
        state_weights.at[shard(f), half],
        own_sems.at[2],
    )
    gives_state = lax.rem(z, NX) == x

    @pl.when(gives_state)
    def _():
        own_state_shard.start()

    pl.semaphore_wait(barrier, devices - 1 + 2 * NX - 1 + 1)

    def give_shard(r, _):
        other = lax.rem(f + r, devices)
        column = NZ * (other // NZ) + lax.rem(2 * x + c + lax.rem(other, NZ), NZ)
        remote(
            w_in.at[:, columns(column)],
            weights.at[0, shard(f), half],
            shard_sems.at[0],
            shard_sems.at[1],
            {"ctx": ctx, "fsdp": other},
        ).start()
        return 0

    def state_shard_copy(r):
        return remote(
            w_in.at[:, columns(STATE_AT // 128 + c)],
            state_weights.at[shard(f), half],
            shard_sems.at[2],
            shard_sems.at[3],
            {"ctx": ctx, "fsdp": lax.rem(f + r, devices)},
        )

    def give_state_shard(r, _):
        state_shard_copy(r).start()
        return 0

    @pl.when(gives_state)
    def _():
        lax.fori_loop(1, devices, give_state_shard, 0)

    lax.fori_loop(1, devices, give_shard, 0)

    def tok_copy(slot, part, dy, target):
        rows = pl.ds(part * (ROWS // 2), ROWS // 2)
        source = tokens.at[rows] if slot == 0 else tok.at[slot, rows]
        way = 0 if dy == 1 else 1
        return remote(
            source,
            tok.at[target, rows],
            tok_send.at[slot, way, part],
            tok_recv.at[target, part],
            at(dy=dy),
        )

    halo_copy = remote(
        tokens.at[pl.ds(ROWS - HALO, HALO)],
        halo,
        halo_sems.at[0],
        halo_sems.at[1],
        {
            "ctx": lax.rem(ctx + (f + 1) // devices, 2 * NX),
            "fsdp": lax.rem(f + 1, devices),
        },
    )
    halo_copy.start()
    tok_copy(0, 0, 1, 3).start()
    tok_copy(0, 1, 3, 1).start()
    tok_copy(0, 1, 1, 3).start()
    tok_copy(0, 0, 3, 1).start()

    upper = (
        lax.broadcasted_iota(jnp.int32, (Q, Q), 0)
        <= lax.broadcasted_iota(jnp.int32, (Q, Q), 1)
    ).astype(BF16)
    for index in range(BLOCKS):
        pair = decay[:, index * Q : (index + 1) * Q]
        cum[index] = jnp.concatenate([pair] * 4, axis=0)
    steps = cum[...].reshape(BLOCKS * 8, Q)
    high, rest = split2(steps)
    lowest = (steps - high.astype(F32) - rest.astype(F32)).astype(BF16)
    total = jnp.dot(lowest, upper, preferred_element_type=F32)
    total = total + jnp.dot(rest, upper, preferred_element_type=F32)
    total = total + jnp.dot(high, upper, preferred_element_type=F32)
    cum[...] = total.reshape(BLOCKS, 8, Q)

    def tok_arrived(slot, part):
        settle(tok.at[slot, pl.ds(part * (ROWS // 2), ROWS // 2)], tok_recv.at[slot, part])

    def x_copy(slot, dx, target, part):
        rows = pl.ds(0, DEPTH) if part is None else pl.ds(part * (DEPTH // 2), DEPTH // 2)
        way = 0 if dx == 1 else 1
        return remote(
            weights.at[slot, rows, half],
            weights.at[target, rows, half],
            x_send.at[slot, way],
            x_recv.at[target, 0 if part is None else part],
            at(dx=dx),
        )

    def core_copy(slot):
        return remote(
            weights.at[slot, :, half],
            weights.at[slot, :, half],
            core_send.at[slot],
            core_recv.at[slot],
            at(dc=1),
        )

    def bc_rows(t, k):
        return lax.rem(y + t, NY) * NZ + lax.rem(z + k, NZ)

    def ring_copy(k, way):
        rows = bc.at[block(bc_rows(0, k))]
        target = (k + 7) % 8 if way == 0 else k + 1
        return remote(
            rows,
            rows,
            ring_send.at[k, way],
            ring_recv.at[target],
            at(dz=1 if way == 0 else NZ - 1),
        )

    def bc_copy(t, k, way):
        index = bc_rows(t, k)
        if t == 0:
            rows, part = bc.at[block(index)], 0
        else:
            part = way
            rows = bc.at[
                pl.ds(pl.multiple_of(index * Q + part * (Q // 2), Q // 2), Q // 2)
            ]
        target = (3 if way == 0 else 1) if t == 0 else 2
        return remote(
            rows,
            rows,
            bc_send.at[t, k, way],
            bc_recv.at[target, k, part],
            at(dy=1 if way == 0 else NY - 1),
        )

    def ring_arrived(k):
        settle(bc.at[block(bc_rows(0, k))], ring_recv.at[k])

    def bc_on(k):
        bc_copy(0, k, 0).start()
        bc_copy(0, k, 1).start()

    def out_piece(t, s, side):
        away = lax.rem(2 * lax.rem(x + s, NX) + side, NZ)
        rows = positions(lax.rem(y + t, NY) * NZ + z)
        return pieces.at[t, s, :, pl.ds(side * 128, 128)], rows, away

    def multiply(t, s):
        product = jnp.dot(tok[t], weights[s], preferred_element_type=F32)
        pieces[t, s] = product.astype(BF16)
        for side in range(2):
            source, rows, away = out_piece(t, s, side)

            @pl.when(away == 0)
            def _():
                pltpu.make_async_copy(source, proj.at[rows], out_send.at[0, t]).start()

            @pl.when(away != 0)
            def _():
                remote(
                    source,
                    proj.at[rows],
                    out_send.at[away, t],
                    out_recv.at[away, t],
                    {"ctx": ctx, "fsdp": y * NZ + lax.rem(z + away, NZ)},
                ).start()

    def core_arrived(slot):
        settle(weights.at[slot, :, other_half], core_recv.at[slot])

    @pl.when(gives_state)
    def _():
        own_state_shard.wait()
        settle(state_weights.at[pl.ds(0, 7 * SHARD), half], shard_sems.at[3])

    @pl.when(jnp.logical_not(gives_state))
    def _():
        settle(state_weights.at[pl.ds(0, 8 * SHARD), half], shard_sems.at[3])

    def give_plane(i, _):
        rows = shard(lax.rem(i, 8) // 2 * NZ + x + NX * lax.rem(i, 2))
        remote(
            state_weights.at[rows, half],
            state_weights.at[rows, half],
            shard_sems.at[4],
            shard_sems.at[5],
            at(dx=1 + i // 8),
        ).start()
        return 0

    lax.fori_loop(0, 24, give_plane, 0)

    settle(state_weights.at[pl.ds(0, 24 * SHARD), half], shard_sems.at[5])
    state_core = remote(
        state_weights.at[:, half],
        state_weights.at[:, half],
        core_send.at[4],
        core_recv.at[4],
        at(dc=1),
    )
    state_core.start()
    own_tokens.wait()
    halo_copy.wait_recv()
    settle(state_weights.at[:, other_half], core_recv.at[4])

    before = jnp.dot(halo[...], state_weights[...], preferred_element_type=F32)
    before = jnp.where(ctx + f == 0, 0.0, before.astype(BF16).astype(F32))
    here = jnp.dot(tok[0], state_weights[...], preferred_element_type=F32)
    window = jnp.concatenate(
        [before[HALO - 8 :], here.astype(BF16).astype(F32)], axis=0
    )
    summed = conv[0:1, STATE_AT:] * window[5 : 5 + ROWS]
    for k in range(1, 4):
        summed = summed + conv[k : k + 1, STATE_AT:] * window[5 + k : 5 + k + ROWS]
    bc[block(f), :] = jax.nn.silu(summed).astype(BF16)

    ring_copy(0, 0).start()
    ring_copy(0, 1).start()
    own_shard.wait()
    settle(
        weights.at[0, pl.ds(0, (devices - 1) * SHARD), half], shard_sems.at[1]
    )
    core_copy(0).start()
    x_copy(0, 1, 3, None).start()
    x_copy(0, 3, 1, None).start()

    tok_arrived(3, 0)
    tok_copy(3, 0, 1, 2).start()
    tok_arrived(1, 1)
    tok_copy(1, 1, 3, 2).start()

    ring_arrived(7)
    ring_copy(7, 0).start()
    ring_arrived(1)
    ring_copy(1, 1).start()
    core_arrived(0)
    multiply(0, 0)
    bc_on(0)
    bc_on(7)
    bc_on(1)
    ring_arrived(6)
    ring_copy(6, 0).start()
    ring_arrived(2)
    ring_copy(2, 1).start()
    bc_on(6)
    bc_on(2)
    ring_arrived(5)
    ring_copy(5, 0).start()
    ring_arrived(3)
    bc_on(5)
    bc_on(3)
    ring_arrived(4)
    bc_on(4)
    tok_arrived(3, 1)
    multiply(3, 0)
    tok_arrived(1, 0)
    multiply(1, 0)
    settle(weights.at[3, :, half], x_recv.at[3, 0])
    x_copy(3, 1, 2, 0).start()
    core_copy(3).start()
    settle(weights.at[1, :, half], x_recv.at[1, 0])
    x_copy(1, 3, 2, 1).start()
    core_copy(1).start()
    core_arrived(3)
    multiply(0, 3)
    multiply(3, 3)
    multiply(1, 3)
    core_arrived(1)
    multiply(0, 1)
    multiply(3, 1)
    multiply(1, 1)
    settle(weights.at[2, pl.ds(0, DEPTH // 2), half], x_recv.at[2, 0])
    settle(weights.at[2, pl.ds(DEPTH // 2, DEPTH // 2), half], x_recv.at[2, 1])
    core_copy(2).start()
    core_arrived(2)
    multiply(0, 2)
    multiply(3, 2)
    multiply(1, 2)
    tok_arrived(2, 0)
    tok_arrived(2, 1)
    multiply(2, 0)
    multiply(2, 3)
    multiply(2, 1)
    multiply(2, 2)

    def heads_arrived(t):
        rows = lax.rem(y + t, NY) * NZ
        settle(proj.at[positions(rows + z)], out_send.at[0, t])
        for away in range(1, NZ):
            source = lax.rem(z + NZ - away, NZ)
            settle(proj.at[positions(rows + source)], out_recv.at[away, t])

    edge = remote(
        proj.at[pl.ds(BLOCKS * Q, HALO)],
        proj.at[pl.ds(0, HALO)],
        edge_sems.at[0],
        edge_sems.at[1],
        {"ctx": lax.rem(ctx + 1, 2 * NX), "fsdp": f},
    )

    def by_position(index):
        rows_of = cum[index]
        both = jnp.concatenate(
            [jnp.broadcast_to(rows_of[h : h + 1], (P_SIZE, Q)) for h in range(2)],
            axis=0,
        )
        return both.T

    def place(i):
        return lax.rem(y + i // NZ, NY) * NZ + lax.rem(i, NZ)

    mine_taps = columns(f)

    def convolve(i, _):
        index = place(i)
        base = pl.multiple_of(index * Q, Q)
        above = proj[pl.ds(base, HALO), :].astype(F32)[HALO - 8 :]
        above = jnp.where(ctx + index == 0, 0.0, above)
        current = proj[positions(index), :].astype(F32)
        window = jnp.concatenate([above, current], axis=0)
        summed = conv[0:1, mine_taps] * window[5 : 5 + Q]
        for k in range(1, 4):
            summed = summed + conv[k : k + 1, mine_taps] * window[5 + k : 5 + k + Q]
        own = jax.nn.silu(summed).astype(BF16)
        inner[pl.ds(base, Q), :] = own
        decays = by_position(index)
        last = decays[Q - 1 : Q]
        scaled = (own.astype(F32) * jnp.exp(last - decays)).astype(BF16)
        b_part = bc[pl.ds(base, Q), :N]
        starts[index] = lax.dot_general(b_part, scaled, TN, preferred_element_type=F32)
        lasts[index] = jnp.broadcast_to(last, (8, WIDTH))
        return 0

    mask = lax.broadcasted_iota(jnp.int32, (Q, Q), 0) >= lax.broadcasted_iota(
        jnp.int32, (Q, Q), 1
    )
    first_head = lane_of((Q, WIDTH)) < P_SIZE

    def inside(i, _):
        index = place(i)
        base = pl.multiple_of(index * Q, Q)
        b_part = bc[pl.ds(base, Q), :N]
        c_part = bc[pl.ds(base, Q), N:]
        own = inner[pl.ds(base, Q), :]
        scores = lax.dot_general(c_part, b_part, NT, preferred_element_type=F32)
        rows_of = cum[index]
        parts = []
        for h in range(2):
            along = rows_of[h : h + 1]
            down = jnp.broadcast_to(along, (WIDTH, Q)).T
            down = jnp.concatenate([down, down], axis=1)
            factors = jnp.exp(jnp.where(mask, down - along, -1e30))
            weighted = (scores * factors).astype(BF16)
            parts.append(jnp.dot(weighted, own, preferred_element_type=F32))
        within[pl.ds(base, Q), :] = jnp.where(first_head, parts[0], parts[1])
        return 0

    def bc_forward(k):
        settle(bc.at[block(bc_rows(3, k))], bc_recv.at[3, k, 0])
        bc_copy(3, k, 0).start()
        settle(bc.at[block(bc_rows(1, k))], bc_recv.at[1, k, 0])
        bc_copy(1, k, 1).start()

    for k in (0, 7, 1, 6, 2, 5, 3, 4):
        bc_forward(k)

    for t in (0, 3, 1):
        heads_arrived(t)

    @pl.when(y != 1)
    def _():
        edge.start()

    @pl.when(jnp.logical_or(y == 0, y == 3))
    def _():
        edge.wait_recv()

    lax.fori_loop(0, 2 * NZ, convolve, 0, unroll=4)
    lax.fori_loop(0, 2 * NZ, inside, 0, unroll=4)

    heads_arrived(2)

    @pl.when(y == 1)
    def _():
        edge.start()

    for k in range(8):
        index = bc_rows(2, k)
        for way in range(2):
            settle(
                bc.at[pl.ds(pl.multiple_of(index * Q + way * (Q // 2), Q // 2), Q // 2)],
                bc_recv.at[2, k, way],
            )

    @pl.when(jnp.logical_or(y == 1, y == 2))
    def _():
        edge.wait_recv()

    lax.fori_loop(2 * NZ, 4 * NZ, convolve, 0, unroll=4)

    def follow(index, carry):
        state, offset = carry
        added = starts[index]
        last = lasts[index, 0:1]
        starts[index] = state
        offsets[index] = jnp.broadcast_to(offset, (8, WIDTH))
        return jnp.exp(last) * state + added, offset + last

    state, offset = lax.fori_loop(
        0,
        BLOCKS,
        follow,
        (jnp.zeros((N, WIDTH), F32), jnp.zeros((1, WIDTH), F32)),
        unroll=2,
    )
    mine[0:N] = state
    mine[N : N + 8] = jnp.broadcast_to(jnp.exp(offset), (8, WIDTH))

    def carry_copy(r):
        return remote(
            mine,
            carries.at[r - 1],
            carry_send.at[r - 1],
            carry_recv.at[r - 1],
            {"ctx": lax.rem(ctx + r, 2 * NX), "fsdp": f},
        )

    for r in range(1, 2 * NX):
        carry_copy(r).start()
    lax.fori_loop(2 * NZ, 4 * NZ, inside, 0, unroll=4)
    for r in range(1, 2 * NX):
        carry_copy(r).wait_recv()
    carried = jnp.zeros((N, WIDTH), F32)
    for r in range(2 * NX - 1, 0, -1):
        new = carries[r - 1, N : N + 1] * carried + carries[r - 1, 0:N]
        carried = jnp.where(ctx - r >= 0, new, carried)

    same_head = (
        lax.broadcasted_iota(jnp.int32, (2 * N, WIDTH), 0) % WIDTH // P_SIZE
        == lane_of((2 * N, WIDTH)) // P_SIZE
    )
    averaging = jnp.where(same_head, 1.0 / P_SIZE, 0.0).astype(BF16)

    def finish(index, _):
        base = pl.multiple_of(index * Q, Q)
        c_part = bc[pl.ds(base, Q), N:]
        start = starts[index] + jnp.exp(offsets[index, 0:1]) * carried
        from_state = jnp.dot(
            jnp.concatenate([c_part, c_part], axis=1),
            jnp.concatenate(split2(start), axis=0),
            preferred_element_type=F32,
        )
        value = within[pl.ds(base, Q), :] + jnp.exp(by_position(index)) * from_state
        squares = jnp.concatenate(split2(value * value), axis=1)
        mean = jnp.dot(squares, averaging, preferred_element_type=F32)
        normed = value * lax.rsqrt(mean + epsilon) * gain[0:1]
        out[pl.ds(base, Q), :] = normed.astype(BF16)
        return 0

    lax.fori_loop(0, BLOCKS, finish, 0, unroll=4)

    edge.wait_send()
    for r in range(1, 2 * NX):
        carry_copy(r).wait_send()
    for k in range(8):
        for way in range(2):
            bc_copy(0, k, way).wait_send()
            bc_copy(3 if way == 0 else 1, k, way).wait_send()
    for k, way in ((0, 0), (0, 1), (7, 0), (1, 1), (6, 0), (2, 1), (5, 0)):
        ring_copy(k, way).wait_send()
    for slot in range(4):
        core_copy(slot).wait_send()
    state_core.wait_send()
    x_copy(0, 1, 3, None).wait_send()
    x_copy(0, 3, 1, None).wait_send()
    x_copy(3, 1, 2, 0).wait_send()
    x_copy(1, 3, 2, 1).wait_send()
    for part in range(2):
        tok_copy(0, part, 1, 3).wait_send()
        tok_copy(0, part, 3, 1).wait_send()
    tok_copy(3, 0, 1, 2).wait_send()
    tok_copy(1, 1, 3, 2).wait_send()
    halo_copy.wait_send()
    settle(weights.at[0, pl.ds(0, (devices - 1) * SHARD), half], shard_sems.at[0])
    settle(state_weights.at[pl.ds(0, 24 * SHARD), half], shard_sems.at[4])

    @pl.when(gives_state)
    def _():
        settle(
            state_weights.at[pl.ds(0, (devices - 1) * SHARD), half], shard_sems.at[2]
        )

    for t in range(NY):
        for away in range(1, NZ):
            settle(proj.at[positions(0)], out_send.at[away, t])


def layer(tokens, w_in, conv_weight, steps, gain):
    vmem = pl.BlockSpec(memory_space=pltpu.VMEM)
    hbm = pl.BlockSpec(memory_space=pl.ANY)
    dma = pltpu.SemaphoreType.DMA
    rows = BLOCKS * Q
    return pl.pallas_call(
        layer_kernel,
        out_shape=jax.ShapeDtypeStruct((rows, WIDTH), BF16),
        in_specs=[hbm] * 2 + [vmem] * 3,
        out_specs=vmem,
        scratch_shapes=[
            pltpu.VMEM((HALO + rows, WIDTH), BF16),
            pltpu.VMEM((rows, 2 * N), BF16),
            pltpu.VMEM((BLOCKS, 8, Q), F32),
            pltpu.VMEM((rows, WIDTH), BF16),
            pltpu.VMEM((BLOCKS, N, WIDTH), F32),
            pltpu.VMEM((BLOCKS, 8, WIDTH), F32),
            pltpu.VMEM((BLOCKS, 8, WIDTH), F32),
            pltpu.VMEM((rows, WIDTH), F32),
            pltpu.VMEM((N + 8, WIDTH), F32),
            pltpu.VMEM((2 * NX - 1, N + 8, WIDTH), F32),
            pltpu.VMEM((NY, ROWS, DEPTH), BF16),
            pltpu.VMEM((NX, DEPTH, 256), BF16),
            pltpu.VMEM((DEPTH, 2 * N), BF16),
            pltpu.VMEM((NY, NX, ROWS, 256), BF16),
            pltpu.VMEM((HALO, DEPTH), BF16),
            dma((3,)),
            dma((2,)),
            dma((4, 2, 2)),
            dma((4, 2)),
            dma((6,)),
            dma((4, 2)),
            dma((4, 2)),
            dma((5,)),
            dma((5,)),
            dma((8, 2)),
            dma((8,)),
            dma((4, 8, 2)),
            dma((4, 8, 2)),
            dma((8, 4)),
            dma((8, 4)),
            dma((2,)),
            dma((2 * NX - 1,)),
            dma((2 * NX - 1,)),
        ],
        compiler_params=pltpu.CompilerParams(
            collective_id=3, has_side_effects=True, vmem_limit_bytes=56 * 2**20
        ),
    )(tokens, w_in, conv_weight, steps, gain)


def body(tokens, w_in, conv_weight, log_decay, norm_gain):
    return layer(tokens, w_in, conv_weight, log_decay.T, norm_gain.reshape(1, WIDTH))


def solution(mesh):
    placed = (P(("ctx", "fsdp"), None), P("fsdp", None), P(), P("ctx", "fsdp"), P("fsdp"))
    return jax.shard_map(
        body, mesh=mesh, in_specs=placed, out_specs=P("ctx", "fsdp"), check_vma=False
    )
```

```python
import jax
import jax.numpy as jnp
from jax import lax
from jax.experimental import pallas as pl
from jax.experimental.pallas import tpu as pltpu
from jax.sharding import PartitionSpec as P

H = 64
P_SIZE = 64
N = 128
Q = 256
HALO = 16
MESH = pl.DeviceIdType.MESH
F32 = jnp.float32
BF16 = jnp.bfloat16
epsilon = 1e-05

NT = (((1,), (1,)), ((), ()))
TN = (((0,), (0,)), ((), ()))


def split2(v):
    high = v.astype(BF16)
    low = (v - high.astype(F32)).astype(BF16)
    return high, low


def lane_of(shape):
    return lax.broadcasted_iota(jnp.int32, shape, 1)


NX, NY, NZ = 4, 4, 8
ROWS = 256
DEPTH = 2560
SHARD = 80
BLOCKS = NY * NZ
WIDTH = 2 * P_SIZE
STATE_AT = 4096


def layer_kernel(
    tokens,
    w_in,
    conv,
    decay,
    gain,
    out,
    proj,
    bc,
    cum,
    inner,
    starts,
    lasts,
    offsets,
    within,
    mine,
    carries,
    tok,
    weights,
    state_weights,
    pieces,
    halo,
    own_sems,
    halo_sems,
    tok_send,
    tok_recv,
    shard_sems,
    x_send,
    x_recv,
    core_send,
    core_recv,
    ring_send,
    ring_recv,
    bc_send,
    bc_recv,
    out_send,
    out_recv,
    edge_sems,
    carry_send,
    carry_recv,
):
    ctx = lax.axis_index("ctx")
    f = lax.axis_index("fsdp")
    x, c = ctx // 2, lax.rem(ctx, 2)
    y, z = f // NZ, lax.rem(f, NZ)

    def at(dx=0, dc=0, dy=0, dz=0):
        return {
            "ctx": lax.rem(x + dx, NX) * 2 + lax.rem(c + dc, 2),
            "fsdp": lax.rem(y + dy, NY) * NZ + lax.rem(z + dz, NZ),
        }

    def remote(source, target, send_sem, recv_sem, device):
        return pltpu.make_async_remote_copy(
            src_ref=source,
            dst_ref=target,
            send_sem=send_sem,
            recv_sem=recv_sem,
            device_id=device,
            device_id_type=MESH,
        )

    def settle(ref, sem):
        pltpu.make_async_copy(ref, ref, sem).wait()

    def columns(index):
        return pl.ds(pl.multiple_of(index * 128, 128), 128)

    def shard(index):
        return pl.ds(pl.multiple_of(index * SHARD, 16), SHARD)

    def block(index):
        return pl.ds(pl.multiple_of(index * Q, Q), Q)

    def positions(index):
        return pl.ds(pl.multiple_of(index * Q + HALO, HALO), Q)

    half = columns(c)
    other_half = columns(1 - c)
    devices = NY * NZ

    barrier = pltpu.get_barrier_semaphore()

    def greet(device):
        pl.semaphore_signal(barrier, inc=1, device_id=device, device_id_type=MESH)

    def greet_row(r, _):
        greet({"ctx": ctx, "fsdp": lax.rem(f + r, devices)})
        return 0

    lax.fori_loop(1, devices, greet_row, 0)
    for r in range(1, 2 * NX):
        greet({"ctx": lax.rem(ctx + r, 2 * NX), "fsdp": f})
    greet(
        {
            "ctx": lax.rem(ctx + 2 * NX - (devices - f) // devices, 2 * NX),
            "fsdp": lax.rem(f + devices - 1, devices),
        }
    )
    own_tokens = pltpu.make_async_copy(tokens, tok.at[0], own_sems.at[0])
    own_tokens.start()
    own_column = NZ * y + lax.rem(2 * x + c + z, NZ)
    own_shard = pltpu.make_async_copy(
        w_in.at[:, columns(own_column)],
        weights.at[0, shard(f), half],
        own_sems.at[1],
    )
    own_shard.start()
    own_state_shard = pltpu.make_async_copy(
        w_in.at[:, columns(STATE_AT // 128 + c)],
        state_weights.at[shard(f), half],
        own_sems.at[2],
    )
    gives_state = lax.rem(z, NX) == x

    @pl.when(gives_state)
    def _():
        own_state_shard.start()

    pl.semaphore_wait(barrier, devices - 1 + 2 * NX - 1 + 1)

    def give_shard(r, _):
        other = lax.rem(f + r, devices)
        column = NZ * (other // NZ) + lax.rem(2 * x + c + lax.rem(other, NZ), NZ)
        remote(
            w_in.at[:, columns(column)],
            weights.at[0, shard(f), half],
            shard_sems.at[0],
            shard_sems.at[1],
            {"ctx": ctx, "fsdp": other},
        ).start()
        return 0

    def state_shard_copy(r):
        return remote(
            w_in.at[:, columns(STATE_AT // 128 + c)],
            state_weights.at[shard(f), half],
            shard_sems.at[2],
            shard_sems.at[3],
            {"ctx": ctx, "fsdp": lax.rem(f + r, devices)},
        )

    def give_state_shard(r, _):
        state_shard_copy(r).start()
        return 0

    @pl.when(gives_state)
    def _():
        lax.fori_loop(1, devices, give_state_shard, 0)

    lax.fori_loop(1, devices, give_shard, 0)

    def tok_copy(slot, part, dy, target):
        rows = pl.ds(part * (ROWS // 2), ROWS // 2)
        source = tokens.at[rows] if slot == 0 else tok.at[slot, rows]
        way = 0 if dy == 1 else 1
        return remote(
            source,
            tok.at[target, rows],
            tok_send.at[slot, way, part],
            tok_recv.at[target, part],
            at(dy=dy),
        )

    halo_copy = remote(
        tokens.at[pl.ds(ROWS - HALO, HALO)],
        halo,
        halo_sems.at[0],
        halo_sems.at[1],
        {
            "ctx": lax.rem(ctx + (f + 1) // devices, 2 * NX),
            "fsdp": lax.rem(f + 1, devices),
        },
    )
    halo_copy.start()
    tok_copy(0, 0, 1, 3).start()
    tok_copy(0, 1, 3, 1).start()
    tok_copy(0, 1, 1, 3).start()
    tok_copy(0, 0, 3, 1).start()

    upper = (
        lax.broadcasted_iota(jnp.int32, (Q, Q), 0)
        <= lax.broadcasted_iota(jnp.int32, (Q, Q), 1)
    ).astype(BF16)
    for index in range(BLOCKS):
        pair = decay[:, index * Q : (index + 1) * Q]
        cum[index] = jnp.concatenate([pair] * 4, axis=0)
    steps = cum[...].reshape(BLOCKS * 8, Q)
    high, rest = split2(steps)
    lowest = (steps - high.astype(F32) - rest.astype(F32)).astype(BF16)
    total = jnp.dot(lowest, upper, preferred_element_type=F32)
    total = total + jnp.dot(rest, upper, preferred_element_type=F32)
    total = total + jnp.dot(high, upper, preferred_element_type=F32)
    cum[...] = total.reshape(BLOCKS, 8, Q)

    def tok_arrived(slot, part):
        settle(tok.at[slot, pl.ds(part * (ROWS // 2), ROWS // 2)], tok_recv.at[slot, part])

    def x_copy(slot, dx, target, part):
        rows = pl.ds(0, DEPTH) if part is None else pl.ds(part * (DEPTH // 2), DEPTH // 2)
        way = 0 if dx == 1 else 1
        return remote(
            weights.at[slot, rows, half],
            weights.at[target, rows, half],
            x_send.at[slot, way],
            x_recv.at[target, 0 if part is None else part],
            at(dx=dx),
        )

    def core_copy(slot):
        return remote(
            weights.at[slot, :, half],
            weights.at[slot, :, half],
            core_send.at[slot],
            core_recv.at[slot],
            at(dc=1),
        )

    def bc_rows(t, k):
        return lax.rem(y + t, NY) * NZ + lax.rem(z + k, NZ)

    def ring_rows(k, part):
        at_row = bc_rows(0, k) * Q + part * (Q // 2)
        return bc.at[pl.ds(pl.multiple_of(at_row, Q // 2), Q // 2)]

    def ring_part(k, way, part):
        rows = ring_rows(k, part)
        target = (k + 7) % 8 if way == 0 else k + 1
        return remote(
            rows,
            rows,
            ring_send.at[k, way, part],
            ring_recv.at[target, part],
            at(dz=1 if way == 0 else NZ - 1),
        )

    def bc_copy(t, k, way):
        index = bc_rows(t, k)
        if t == 0:
            rows, part = bc.at[block(index)], 0
        else:
            part = way
            rows = bc.at[
                pl.ds(pl.multiple_of(index * Q + part * (Q // 2), Q // 2), Q // 2)
            ]
        target = (3 if way == 0 else 1) if t == 0 else 2
        return remote(
            rows,
            rows,
            bc_send.at[t, k, way],
            bc_recv.at[target, k, part],
            at(dy=1 if way == 0 else NY - 1),
        )

    def ring_arrived(k, part):
        settle(ring_rows(k, part), ring_recv.at[k, part])

    def bc_on(k):
        bc_copy(0, k, 0).start()
        bc_copy(0, k, 1).start()

    def out_piece(t, s, side):
        away = lax.rem(2 * lax.rem(x + s, NX) + side, NZ)
        rows = positions(lax.rem(y + t, NY) * NZ + z)
        return pieces.at[t, s, :, pl.ds(side * 128, 128)], rows, away

    def multiply(t, s):
        product = jnp.dot(tok[t], weights[s], preferred_element_type=F32)
        pieces[t, s] = product.astype(BF16)
        for side in range(2):
            source, rows, away = out_piece(t, s, side)

            @pl.when(away == 0)
            def _():
                pltpu.make_async_copy(source, proj.at[rows], out_send.at[0, t]).start()

            @pl.when(away != 0)
            def _():
                remote(
                    source,
                    proj.at[rows],
                    out_send.at[away, t],
                    out_recv.at[away, t],
                    {"ctx": ctx, "fsdp": y * NZ + lax.rem(z + away, NZ)},
                ).start()

    def core_arrived(slot):
        settle(weights.at[slot, :, other_half], core_recv.at[slot])

    @pl.when(gives_state)
    def _():
        own_state_shard.wait()
        settle(state_weights.at[pl.ds(0, 7 * SHARD), half], shard_sems.at[3])

    @pl.when(jnp.logical_not(gives_state))
    def _():
        settle(state_weights.at[pl.ds(0, 8 * SHARD), half], shard_sems.at[3])

    def give_plane(i, _):
        rows = shard(lax.rem(i, 8) // 2 * NZ + x + NX * lax.rem(i, 2))
        remote(
            state_weights.at[rows, half],
            state_weights.at[rows, half],
            shard_sems.at[4],
            shard_sems.at[5],
            at(dx=1 + i // 8),
        ).start()
        return 0

    lax.fori_loop(0, 24, give_plane, 0)

    settle(state_weights.at[pl.ds(0, 24 * SHARD), half], shard_sems.at[5])
    state_core = remote(
        state_weights.at[:, half],
        state_weights.at[:, half],
        core_send.at[4],
        core_recv.at[4],
        at(dc=1),
    )
    state_core.start()
    own_tokens.wait()
    halo_copy.wait_recv()
    settle(state_weights.at[:, other_half], core_recv.at[4])

    before = jnp.dot(halo[...], state_weights[...], preferred_element_type=F32)
    before = jnp.where(ctx + f == 0, 0.0, before.astype(BF16).astype(F32))
    here = jnp.dot(tok[0], state_weights[...], preferred_element_type=F32)
    window = jnp.concatenate(
        [before[HALO - 8 :], here.astype(BF16).astype(F32)], axis=0
    )
    summed = conv[0:1, STATE_AT:] * window[5 : 5 + ROWS]
    for k in range(1, 4):
        summed = summed + conv[k : k + 1, STATE_AT:] * window[5 + k : 5 + k + ROWS]
    bc[block(f), :] = jax.nn.silu(summed).astype(BF16)

    for part in range(2):
        ring_part(0, 0, part).start()
        ring_part(0, 1, part).start()
    own_shard.wait()
    settle(
        weights.at[0, pl.ds(0, (devices - 1) * SHARD), half], shard_sems.at[1]
    )
    core_copy(0).start()
    x_copy(0, 1, 3, None).start()
    x_copy(0, 3, 1, None).start()

    tok_arrived(3, 0)
    tok_copy(3, 0, 1, 2).start()
    tok_arrived(1, 1)
    tok_copy(1, 1, 3, 2).start()

    for part in range(2):
        ring_arrived(7, part)
        ring_part(7, 0, part).start()
        ring_arrived(1, part)
        ring_part(1, 1, part).start()
    core_arrived(0)
    multiply(0, 0)
    bc_on(0)
    bc_on(7)
    bc_on(1)
    for part in range(2):
        ring_arrived(6, part)
        ring_part(6, 0, part).start()
        ring_arrived(2, part)
        ring_part(2, 1, part).start()
    bc_on(6)
    bc_on(2)
    for part in range(2):
        ring_arrived(5, part)
        ring_part(5, 0, part).start()
        ring_arrived(3, part)
    bc_on(5)
    bc_on(3)
    ring_arrived(4, 0)
    ring_arrived(4, 1)
    bc_on(4)
    tok_arrived(3, 1)
    multiply(3, 0)
    tok_arrived(1, 0)
    multiply(1, 0)
    settle(weights.at[3, :, half], x_recv.at[3, 0])
    x_copy(3, 1, 2, 0).start()
    core_copy(3).start()
    settle(weights.at[1, :, half], x_recv.at[1, 0])
    x_copy(1, 3, 2, 1).start()
    core_copy(1).start()
    core_arrived(3)
    multiply(0, 3)
    multiply(3, 3)
    multiply(1, 3)
    core_arrived(1)
    multiply(0, 1)
    multiply(3, 1)
    multiply(1, 1)
    settle(weights.at[2, pl.ds(0, DEPTH // 2), half], x_recv.at[2, 0])
    settle(weights.at[2, pl.ds(DEPTH // 2, DEPTH // 2), half], x_recv.at[2, 1])
    core_copy(2).start()
    core_arrived(2)
    multiply(0, 2)
    multiply(3, 2)
    multiply(1, 2)
    tok_arrived(2, 0)
    tok_arrived(2, 1)
    multiply(2, 0)
    multiply(2, 3)
    multiply(2, 1)
    multiply(2, 2)

    def heads_arrived(t):
        rows = lax.rem(y + t, NY) * NZ
        settle(proj.at[positions(rows + z)], out_send.at[0, t])
        for away in range(1, NZ):
            source = lax.rem(z + NZ - away, NZ)
            settle(proj.at[positions(rows + source)], out_recv.at[away, t])

    edge = remote(
        proj.at[pl.ds(BLOCKS * Q, HALO)],
        proj.at[pl.ds(0, HALO)],
        edge_sems.at[0],
        edge_sems.at[1],
        {"ctx": lax.rem(ctx + 1, 2 * NX), "fsdp": f},
    )

    def by_position(index):
        rows_of = cum[index]
        both = jnp.concatenate(
            [jnp.broadcast_to(rows_of[h : h + 1], (P_SIZE, Q)) for h in range(2)],
            axis=0,
        )
        return both.T

    def place(i):
        return lax.rem(y + i // NZ, NY) * NZ + lax.rem(i, NZ)

    mine_taps = columns(f)

    def convolve(i, _):
        index = place(i)
        base = pl.multiple_of(index * Q, Q)
        above = proj[pl.ds(base, HALO), :].astype(F32)[HALO - 8 :]
        above = jnp.where(ctx + index == 0, 0.0, above)
        current = proj[positions(index), :].astype(F32)
        window = jnp.concatenate([above, current], axis=0)
        summed = conv[0:1, mine_taps] * window[5 : 5 + Q]
        for k in range(1, 4):
            summed = summed + conv[k : k + 1, mine_taps] * window[5 + k : 5 + k + Q]
        own = jax.nn.silu(summed).astype(BF16)
        inner[pl.ds(base, Q), :] = own
        decays = by_position(index)
        last = decays[Q - 1 : Q]
        scaled = (own.astype(F32) * jnp.exp(last - decays)).astype(BF16)
        b_part = bc[pl.ds(base, Q), :N]
        starts[index] = lax.dot_general(b_part, scaled, TN, preferred_element_type=F32)
        lasts[index] = jnp.broadcast_to(last, (8, WIDTH))
        return 0

    mask = lax.broadcasted_iota(jnp.int32, (Q, Q), 0) >= lax.broadcasted_iota(
        jnp.int32, (Q, Q), 1
    )
    first_head = lane_of((Q, WIDTH)) < P_SIZE

    def inside(i, _):
        index = place(i)
        base = pl.multiple_of(index * Q, Q)
        b_part = bc[pl.ds(base, Q), :N]
        c_part = bc[pl.ds(base, Q), N:]
        own = inner[pl.ds(base, Q), :]
        scores = lax.dot_general(c_part, b_part, NT, preferred_element_type=F32)
        rows_of = cum[index]
        parts = []
        for h in range(2):
            along = rows_of[h : h + 1]
            down = jnp.broadcast_to(along, (WIDTH, Q)).T
            down = jnp.concatenate([down, down], axis=1)
            factors = jnp.exp(jnp.where(mask, down - along, -1e30))
            weighted = (scores * factors).astype(BF16)
            parts.append(jnp.dot(weighted, own, preferred_element_type=F32))
        within[pl.ds(base, Q), :] = jnp.where(first_head, parts[0], parts[1])
        return 0

    def bc_forward(k):
        settle(bc.at[block(bc_rows(3, k))], bc_recv.at[3, k, 0])
        bc_copy(3, k, 0).start()
        settle(bc.at[block(bc_rows(1, k))], bc_recv.at[1, k, 0])
        bc_copy(1, k, 1).start()

    for k in (0, 7, 1, 6, 2, 5, 3, 4):
        bc_forward(k)

    for t in (0, 3, 1):
        heads_arrived(t)

    @pl.when(y != 1)
    def _():
        edge.start()

    @pl.when(jnp.logical_or(y == 0, y == 3))
    def _():
        edge.wait_recv()

    lax.fori_loop(0, 2 * NZ, convolve, 0, unroll=4)
    lax.fori_loop(0, 2 * NZ, inside, 0, unroll=4)

    heads_arrived(2)

    @pl.when(y == 1)
    def _():
        edge.start()

    @pl.when(jnp.logical_or(y == 1, y == 2))
    def _():
        edge.wait_recv()

    lax.fori_loop(3 * NZ, 4 * NZ, convolve, 0, unroll=4)
    lax.fori_loop(3 * NZ, 4 * NZ, inside, 0, unroll=4)
    for k in range(8):
        index = bc_rows(2, k)
        for way in range(2):
            settle(
                bc.at[pl.ds(pl.multiple_of(index * Q + way * (Q // 2), Q // 2), Q // 2)],
                bc_recv.at[2, k, way],
            )

    lax.fori_loop(2 * NZ, 3 * NZ, convolve, 0, unroll=8)

    def follow(index, carry):
        state, offset = carry
        added = starts[index]
        last = lasts[index, 0:1]
        starts[index] = state
        offsets[index] = jnp.broadcast_to(offset, (8, WIDTH))
        return jnp.exp(last) * state + added, offset + last

    state, offset = lax.fori_loop(
        0,
        BLOCKS,
        follow,
        (jnp.zeros((N, WIDTH), F32), jnp.zeros((1, WIDTH), F32)),
        unroll=2,
    )
    mine[0:N] = state.astype(BF16)
    fall = split2(jnp.exp(offset))
    mine[N : N + HALO] = jnp.concatenate(
        [jnp.broadcast_to(part, (HALO // 2, WIDTH)) for part in fall], axis=0
    )

    def carry_copy(r):
        return remote(
            mine,
            carries.at[r - 1],
            carry_send.at[r - 1],
            carry_recv.at[r - 1],
            {"ctx": lax.rem(ctx + r, 2 * NX), "fsdp": f},
        )

    for r in range(1, 2 * NX):
        carry_copy(r).start()
    lax.fori_loop(2 * NZ, 3 * NZ, inside, 0, unroll=4)
    for r in range(1, 2 * NX):
        carry_copy(r).wait_recv()
    carried = jnp.zeros((N, WIDTH), F32)
    for r in range(2 * NX - 1, 0, -1):
        fall = carries[r - 1, N : N + HALO].astype(F32)
        fall = fall[0:1] + fall[HALO // 2 : HALO // 2 + 1]
        new = fall * carried + carries[r - 1, 0:N].astype(F32)
        carried = jnp.where(ctx - r >= 0, new, carried)

    same_head = (
        lax.broadcasted_iota(jnp.int32, (2 * N, WIDTH), 0) % WIDTH // P_SIZE
        == lane_of((2 * N, WIDTH)) // P_SIZE
    )
    averaging = jnp.where(same_head, 1.0 / P_SIZE, 0.0).astype(BF16)

    def finish(index, _):
        base = pl.multiple_of(index * Q, Q)
        c_part = bc[pl.ds(base, Q), N:]
        start = starts[index] + jnp.exp(offsets[index, 0:1]) * carried
        from_state = jnp.dot(
            jnp.concatenate([c_part, c_part], axis=1),
            jnp.concatenate(split2(start), axis=0),
            preferred_element_type=F32,
        )
        value = within[pl.ds(base, Q), :] + jnp.exp(by_position(index)) * from_state
        squares = jnp.concatenate(split2(value * value), axis=1)
        mean = jnp.dot(squares, averaging, preferred_element_type=F32)
        normed = value * lax.rsqrt(mean + epsilon) * gain[0:1]
        inner[pl.ds(base, Q), :] = normed.astype(BF16)
        pltpu.make_async_copy(
            inner.at[pl.ds(base, Q)], out.at[pl.ds(base, Q)], own_sems.at[3]
        ).start()
        return 0

    lax.fori_loop(0, BLOCKS, finish, 0, unroll=8)
    settle(inner, own_sems.at[3])

    edge.wait_send()
    for r in range(1, 2 * NX):
        carry_copy(r).wait_send()
    for k in range(8):
        for way in range(2):
            bc_copy(0, k, way).wait_send()
            bc_copy(3 if way == 0 else 1, k, way).wait_send()
    for k, way in ((0, 0), (0, 1), (7, 0), (1, 1), (6, 0), (2, 1), (5, 0)):
        ring_part(k, way, 0).wait_send()
        ring_part(k, way, 1).wait_send()
    for slot in range(4):
        core_copy(slot).wait_send()
    state_core.wait_send()
    x_copy(0, 1, 3, None).wait_send()
    x_copy(0, 3, 1, None).wait_send()
    x_copy(3, 1, 2, 0).wait_send()
    x_copy(1, 3, 2, 1).wait_send()
    for part in range(2):
        tok_copy(0, part, 1, 3).wait_send()
        tok_copy(0, part, 3, 1).wait_send()
    tok_copy(3, 0, 1, 2).wait_send()
    tok_copy(1, 1, 3, 2).wait_send()
    halo_copy.wait_send()
    settle(weights.at[0, pl.ds(0, (devices - 1) * SHARD), half], shard_sems.at[0])
    settle(state_weights.at[pl.ds(0, 24 * SHARD), half], shard_sems.at[4])

    @pl.when(gives_state)
    def _():
        settle(
            state_weights.at[pl.ds(0, (devices - 1) * SHARD), half], shard_sems.at[2]
        )

    for t in range(NY):
        for away in range(1, NZ):
            settle(proj.at[positions(0)], out_send.at[away, t])


def layer(tokens, w_in, conv_weight, steps, gain):
    vmem = pl.BlockSpec(memory_space=pltpu.VMEM)
    hbm = pl.BlockSpec(memory_space=pl.ANY)
    dma = pltpu.SemaphoreType.DMA
    rows = BLOCKS * Q
    return pl.pallas_call(
        layer_kernel,
        out_shape=jax.ShapeDtypeStruct((rows, WIDTH), BF16),
        in_specs=[hbm] * 2 + [vmem] * 3,
        out_specs=hbm,
        scratch_shapes=[
            pltpu.VMEM((HALO + rows, WIDTH), BF16),
            pltpu.VMEM((rows, 2 * N), BF16),
            pltpu.VMEM((BLOCKS, 8, Q), F32),
            pltpu.VMEM((rows, WIDTH), BF16),
            pltpu.VMEM((BLOCKS, N, WIDTH), F32),
            pltpu.VMEM((BLOCKS, 8, WIDTH), F32),
            pltpu.VMEM((BLOCKS, 8, WIDTH), F32),
            pltpu.VMEM((rows, WIDTH), F32),
            pltpu.VMEM((N + HALO, WIDTH), BF16),
            pltpu.VMEM((2 * NX - 1, N + HALO, WIDTH), BF16),
            pltpu.VMEM((NY, ROWS, DEPTH), BF16),
            pltpu.VMEM((NX, DEPTH, 256), BF16),
            pltpu.VMEM((DEPTH, 2 * N), BF16),
            pltpu.VMEM((NY, NX, ROWS, 256), BF16),
            pltpu.VMEM((HALO, DEPTH), BF16),
            dma((4,)),
            dma((2,)),
            dma((4, 2, 2)),
            dma((4, 2)),
            dma((6,)),
            dma((4, 2)),
            dma((4, 2)),
            dma((5,)),
            dma((5,)),
            dma((8, 2, 2)),
            dma((8, 2)),
            dma((4, 8, 2)),
            dma((4, 8, 2)),
            dma((8, 4)),
            dma((8, 4)),
            dma((2,)),
            dma((2 * NX - 1,)),
            dma((2 * NX - 1,)),
        ],
        compiler_params=pltpu.CompilerParams(
            collective_id=3, has_side_effects=True, vmem_limit_bytes=56 * 2**20
        ),
    )(tokens, w_in, conv_weight, steps, gain)


def body(tokens, w_in, conv_weight, log_decay, norm_gain):
    return layer(tokens, w_in, conv_weight, log_decay.T, norm_gain.reshape(1, WIDTH))


def solution(mesh):
    placed = (P(("ctx", "fsdp"), None), P("fsdp", None), P(), P("ctx", "fsdp"), P("fsdp"))
    return jax.shard_map(
        body, mesh=mesh, in_specs=placed, out_specs=P("ctx", "fsdp"), check_vma=False
    )
```
